128 devices in a mesh: fsdp: 128 (over x, y, z, core).
Axes of the slice: x: 4, y: 4, z: 4, core: 2. Of those that a mesh axis runs over, the one named last changes fastest.
Arguments:
- hidden_in: bfloat16 [65536, 768], P('fsdp'), may hold values from -6 to 6
- out_cotangent: bfloat16 [65536, 768], P('fsdp'), may hold values from -6 to 6
- lengths: int32 [256], replicated, may hold values from 1 to 511, as said below
- assignment: int32 [256], replicated, may hold values from 0 to 127
- qkv_weight: bfloat16 [768, 2304], P('fsdp'), may hold values from -0.21875 to 0.21875
- query_bias: bfloat16 [768], P('fsdp'), may hold values from -3 to 3
- value_bias: bfloat16 [768], P('fsdp'), may hold values from -3 to 3
- out_weight: bfloat16 [768, 768], P('fsdp'), may hold values from -2.5 to 2.5
- out_bias: bfloat16 [768], P('fsdp'), may hold values from -3 to 3
- first_gain: bfloat16 [768], P('fsdp'), may hold values from 0.5 to 1.5
- first_shift: bfloat16 [768], P('fsdp'), may hold values from -3 to 3
- in_weight: bfloat16 [768, 3072], P('fsdp'), may hold values from -0.21875 to 0.21875
- in_bias: bfloat16 [3072], P('fsdp'), may hold values from -3 to 3
- back_weight: bfloat16 [3072, 768], P('fsdp'), may hold values from -0.109375 to 0.109375
- back_bias: bfloat16 [768], P('fsdp'), may hold values from -3 to 3
- second_gain: bfloat16 [768], P('fsdp'), may hold values from 0.5 to 1.5
- second_shift: bfloat16 [768], P('fsdp'), may hold values from -3 to 3
Outputs:
- layer_out: bfloat16 [65536, 768], P('fsdp')
- input_grad: bfloat16 [65536, 768], P('fsdp')
- qkv_weight_grad: float32 [768, 2304], P('fsdp')
- query_bias_grad: float32 [768], P('fsdp')
- value_bias_grad: float32 [768], P('fsdp')
- out_weight_grad: float32 [768, 768], P('fsdp')
- out_bias_grad: float32 [768], P('fsdp')
- first_gain_grad: float32 [768], P('fsdp')
- first_shift_grad: float32 [768], P('fsdp')
- in_weight_grad: float32 [768, 3072], P('fsdp')
- in_bias_grad: float32 [3072], P('fsdp')
- back_weight_grad: float32 [3072, 768], P('fsdp')
- back_bias_grad: float32 [768], P('fsdp')
- second_gain_grad: float32 [768], P('fsdp')
- second_shift_grad: float32 [768], P('fsdp')
The draws below stay inside these ranges and needn't reach their ends.
Inputs may be any that keep to these rules, and one draw needn't show every extreme that they name: Each device holds exactly 2 sequences; the lengths on one device sum to at most 512, and to exactly 512 on some device.
All inputs are finite; a program needn't handle non-finite values.
Results may differ from the reference program's by a relative error of at most 0.018.
Values may be sent and summed in bfloat16 or wider, within the bound.
No kernel may reach another device: no remote copies, remote signals or barrier semaphores. Data moves between devices by JAX's collectives and lax.ppermute only.
A program may use at most 192 MiB of HBM per device.

```python
import jax
import jax.numpy as jnp
from jax import lax

D = 768
HEADS = 12
HD = 64
FF = 3072
SLOT = 512
SEQ_DEV = 2
TOKENS = 65536
SEQS = 256
N_FSDP = 128


def pack_draw(key):
    count_dev = SEQS // SEQ_DEV
    key_load, key_full, key_first, key_order = jax.random.split(key, 4)
    devices = jnp.arange(count_dev, dtype=jnp.int32)
    loads = jax.random.randint(key_load, (count_dev,), SLOT // 4, SLOT + 1)
    fullest = jax.random.randint(key_full, (), 0, count_dev)
    loads = jnp.where(devices == fullest, SLOT, loads)
    firsts = jax.random.randint(key_first, (count_dev,), 1, loads)
    firsts = jnp.where(devices == fullest, 1, firsts)
    pieces = jnp.stack([firsts, loads - firsts], axis=1).reshape(-1).astype(jnp.int32)
    order = jax.random.permutation(key_order, SEQS)
    owners = (jnp.arange(SEQS, dtype=jnp.int32) // SEQ_DEV).astype(jnp.int32)
    lengths = jnp.zeros((SEQS,), jnp.int32).at[order].set(pieces)
    owner_of = jnp.zeros((SEQS,), jnp.int32).at[order].set(owners)
    return (lengths, owner_of)


def draw_lengths(key, part):
    return pack_draw(key)[0]


def draw_assignment(key, part):
    return pack_draw(key)[1]


def block_scale(rng, dims, cuts, low, high):
    loudness, own = 1.0, jax.random.fold_in(rng, 6)
    for axis_at, blocks in cuts:
        steps = jnp.exp(jax.random.uniform(jax.random.fold_in(own, axis_at), (blocks,), jnp.float32, low / len(cuts), high / len(cuts)))
        loudness = loudness * jnp.repeat(steps, dims[axis_at] // blocks).reshape([-1 if axis == axis_at else 1 for axis in range(len(dims))])
    return loudness


def scatter_about(rng, extent, spread, most, cuts=(), kind=jnp.bfloat16):
    factor_of = block_scale(rng, extent, cuts, -0.22, 0.18) if cuts else 1.0
    drawn = jax.random.normal(rng, extent, jnp.float32) * spread * factor_of
    return jnp.minimum(jnp.maximum(drawn, -most), most).astype(kind)


def setup_inputs(seed: int = 0) -> dict:
    seeds = jax.random.split(jax.random.key(seed), 18)
    hidden_in = scatter_about(seeds[0], (TOKENS, D), 1.0, 6.0, ((0, 128),))
    out_cotangent = scatter_about(seeds[1], (TOKENS, D), 1.0, 6.0, ((0, 128),))
    lengths = draw_lengths(jax.random.fold_in(seeds[17], 71), 0)
    assignment = draw_assignment(jax.random.fold_in(seeds[17], 71), 0)
    qkv_weight = scatter_about(seeds[4], (D, 3 * D), D ** -0.5, 0.21875, ((0, 128),))
    query_bias = scatter_about(seeds[5], (D,), 0.5, 3.0, ((0, 128),))
    value_bias = scatter_about(seeds[6], (D,), 0.5, 3.0, ((0, 128),))
    out_weight = scatter_about(seeds[7], (D, D), (D * 4 // SLOT) ** -0.5, 2.5, ((0, 128),))
    out_bias = scatter_about(seeds[8], (D,), 0.5, 3.0, ((0, 128),))
    first_gain = jnp.clip(1.0 + 0.1 * jax.random.normal(seeds[9], (D,), jnp.float32), 0.5, 1.5).astype(jnp.bfloat16)
    first_shift = scatter_about(seeds[10], (D,), 0.5, 3.0, ((0, 128),))
    in_weight = scatter_about(seeds[11], (D, FF), D ** -0.5, 0.21875, ((0, 128),))
    in_bias = scatter_about(seeds[12], (FF,), 0.5, 3.0, ((0, 128),))
    back_weight = scatter_about(seeds[13], (FF, D), FF ** -0.5, 0.109375, ((0, 128),))
    back_bias = scatter_about(seeds[14], (D,), 0.5, 3.0, ((0, 128),))
    second_gain = jnp.clip(1.0 + 0.1 * jax.random.normal(seeds[15], (D,), jnp.float32), 0.5, 1.5).astype(jnp.bfloat16)
    second_shift = scatter_about(seeds[16], (D,), 0.5, 3.0, ((0, 128),))
    return {"hidden_in": hidden_in, "out_cotangent": out_cotangent, "lengths": lengths, "assignment": assignment, "qkv_weight": qkv_weight, "query_bias": query_bias, "value_bias": value_bias, "out_weight": out_weight, "out_bias": out_bias, "first_gain": first_gain, "first_shift": first_shift, "in_weight": in_weight, "in_bias": in_bias, "back_weight": back_weight, "back_bias": back_bias, "second_gain": second_gain, "second_shift": second_shift}


@jax.custom_vjp
def low(v):
    return lax.optimization_barrier(v.astype(jnp.bfloat16)).astype(jnp.float32)

@jax.custom_vjp
def low_back(v):
    return v

def low_keep(v):
    return (low(v), None)

def low_pass(kept, grad):
    return (grad,)

def back_keep(v):
    return (v, None)

def back_low(kept, grad):
    return (low(grad),)
low.defvjp(low_keep, low_pass)
low_back.defvjp(back_keep, back_low)
EPSILON = 1e-05
SCALE = 0.125
MASK_FILL = -1000000000.0
HIGH = lax.Precision.HIGHEST

def layer_norm(total, gain, shift):
    centre = lax.optimization_barrier(jnp.mean(total, axis=-1, keepdims=True))
    centred = total - centre
    variance = lax.optimization_barrier(jnp.mean(centred * centred, axis=-1, keepdims=True))
    return centred * lax.rsqrt(variance + EPSILON) * gain + shift

def segments_all(lengths, assignment):
    count = lengths.shape[0]
    order = jnp.arange(count, dtype=jnp.int32)
    same = assignment[:, None] == assignment[None, :]
    before = order[None, :] < order[:, None]
    offset = lax.optimization_barrier(jnp.sum(jnp.where(same & before, lengths[None, :], 0), axis=1)).astype(jnp.int32)
    devices = jnp.arange(N_FSDP, dtype=jnp.int32)[:, None, None]
    places = jnp.arange(SLOT, dtype=jnp.int32)[None, :, None]
    inside = (assignment[None, None, :] == devices) & (places >= offset[None, None, :]) & (places < (offset + lengths)[None, None, :])
    return lax.optimization_barrier(jnp.sum(jnp.where(inside, order[None, None, :] + 1, 0), axis=-1)).astype(jnp.int32)

def attend_block(block):
    query_part, key_part, value_part, segment_part = block
    raw = jnp.einsum('qhd,khd->hqk', query_part, key_part, precision=HIGH) * SCALE
    allowed = segment_part[:, None] == segment_part[None, :]
    scores = low_back(jnp.where(allowed[None], raw, MASK_FILL))
    top = lax.optimization_barrier(jnp.max(scores, axis=-1, keepdims=True))
    logsum = top + jnp.log(lax.optimization_barrier(jnp.sum(jnp.exp(scores - top), axis=-1, keepdims=True)))
    probs = jnp.exp(scores - logsum)
    return jnp.einsum('hqk,khd->qhd', low(probs), value_part, precision=HIGH)

def reference(hidden_in, out_cotangent, lengths, assignment, qkv_weight, query_bias, value_bias, out_weight, out_bias, first_gain, first_shift, in_weight, in_bias, back_weight, back_bias, second_gain, second_shift):
    segment = segments_all(lengths, assignment)
    valid = (segment > 0).astype(jnp.float32).reshape(TOKENS, 1)

    def forward(inputs, w_qkv, b_query, b_value, w_out, b_out, gain_one, shift_one, w_in, b_in, w_back, b_back, gain_two, shift_two):
        mixed = jnp.dot(inputs, w_qkv, precision=HIGH)
        query = low_back(low(mixed[:, :D] + b_query))
        keys = low_back(low(mixed[:, D:2 * D]))
        values = low_back(low(mixed[:, 2 * D:] + b_value))
        shape = (N_FSDP, SLOT, HEADS, HD)
        context = lax.map(jax.checkpoint(attend_block), (query.reshape(shape), keys.reshape(shape), values.reshape(shape), segment))
        context = low_back(low(context.reshape(TOKENS, D)))
        attn = low_back(jnp.dot(context, w_out, precision=HIGH) + b_out)
        first_norm = layer_norm(inputs + attn, gain_one, shift_one)
        first_low = low(first_norm)
        pre = low_back(jnp.dot(first_low, w_in, precision=HIGH) + b_in)
        act = low(jax.nn.gelu(pre, approximate=False))
        branch = low_back(jnp.dot(act, w_back, precision=HIGH) + b_back)
        return layer_norm(first_norm + branch, gain_two, shift_two) * valid
    params = (qkv_weight, query_bias, value_bias, out_weight, out_bias, first_gain, first_shift, in_weight, in_bias, back_weight, back_bias, second_gain, second_shift)
    floats = [p.astype(jnp.float32) for p in params]
    result, pullback = jax.vjp(forward, hidden_in.astype(jnp.float32), *floats)
    grads = pullback(out_cotangent.astype(jnp.float32))
    return (result.astype(jnp.bfloat16), grads[0].astype(jnp.bfloat16), grads[1], grads[2], grads[3], grads[4], grads[5], grads[6], grads[7], grads[8], grads[9], grads[10], grads[11], grads[12], grads[13])
```

```python
import jax
import jax.numpy as jnp
from jax import lax
from jax.sharding import Mesh, PartitionSpec as P

HEADS = 12
D = 768
FF = 3072
LANES = 128
GROUP = 8
ROWS_A = 880
ROWS_ALL = 1744
EPSILON = 1e-05
SCALE = 0.125
MASK_FILL = -1000000000.0
bf16, f32 = jnp.bfloat16, jnp.float32


def shifted(n, step):
    return [(i, (i + step) % n) for i in range(n)]


def blocks_of(w, half):
    rows, cols = w.shape
    part = w[:, half * (cols // 2) : (half + 1) * (cols // 2)]
    return jnp.moveaxis(part.reshape(rows, -1, LANES), 1, 0)


def gather_all(qkv, out, inw, back, small):
    core = lax.axis_index("c")
    halves = []
    for half in range(2):
        wide = jnp.concatenate([blocks_of(w, half) for w in (qkv, out, inw)], axis=0)
        halves.append(wide.reshape(-1, LANES))
        halves.append(blocks_of(back, half).reshape(-1, LANES))
    row = jnp.concatenate(small + [jnp.zeros((LANES - 72,), bf16)])[None]
    packed = jnp.concatenate(halves + [row, jnp.zeros((15, LANES), bf16)], axis=0)
    near = lax.all_gather(packed, ("z", "c"), tiled=False)
    mine = lax.dynamic_slice_in_dim(near, core * 216, 216, axis=1)
    wide = jnp.moveaxis(mine[:, :144].reshape(GROUP, 24, 6, LANES), 0, 1).reshape(-1, LANES)
    tall = jnp.moveaxis(mine[:, 144:].reshape(GROUP, 3, 24, LANES), 0, 1).reshape(-1, LANES)
    tail = jnp.pad(near[:, 432], ((0, 8), (0, 0)))
    block = jnp.concatenate([wide, tall, tail], axis=0)
    return lax.all_gather(block, ("x", "y", "c"), tiled=False).reshape(16, 2, ROWS_ALL, LANES)


def wide_of(gathered, first, count):
    part = gathered[:, :, first * 48 : (first + count) * 48].reshape(16, 2, count, 48, LANES)
    return part.transpose(0, 3, 1, 2, 4).reshape(D, 2 * count * LANES)


def unpack(gathered):
    qkv, out, inw = (wide_of(gathered, a, b) for a, b in ((0, 9), (9, 3), (12, 12)))
    back = gathered[:, :, 1152:1728].reshape(16, 2, 3, 192, LANES)
    back = back.transpose(0, 3, 1, 2, 4).reshape(FF, D)
    small = gathered[:, 0, 1728:1736, :72].reshape(128, 72)
    cuts = (6, 6, 6, 6, 6, 24, 6, 6, 6)
    vectors, at = [], 0
    for cut in cuts:
        vectors.append(small[:, at : at + cut].reshape(-1))
        at += cut
    return qkv, out, inw, back, vectors


def pack_wide(grad, count):
    part = grad.astype(bf16).reshape(16, 48, 2, count, LANES)
    return part.transpose(0, 2, 3, 1, 4).reshape(16, 2, count * 48, LANES)


def pack(qkv, out, inw, back, vectors):
    tall = back.astype(bf16).reshape(16, 192, 2, 3, LANES).transpose(0, 2, 3, 1, 4)
    rows = jnp.concatenate([v.astype(bf16).reshape(128, -1) for v in vectors], axis=1)
    rows = jnp.pad(rows, ((0, 0), (0, LANES - 72))).reshape(16, GROUP, LANES)
    rows = jnp.pad(rows, ((0, 0), (0, 8), (0, 0)))
    rows = jnp.broadcast_to(rows[:, None], (16, 2, 16, LANES))
    wide = [pack_wide(g, n) for g, n in ((qkv, 9), (out, 3), (inw, 12))]
    return jnp.concatenate(wide + [tall.reshape(16, 2, 576, LANES), rows], axis=2)


def axis_sum(value, dim, axis):
    place = lax.axis_index(axis)
    total = lax.dynamic_index_in_dim(value, place, dim, keepdims=False).astype(f32)
    arrived = [
        lax.ppermute(
            lax.dynamic_index_in_dim(value, (place + k) % 4, dim, keepdims=False),
            axis,
            shifted(4, k),
        )
        for k in (1, 3, 2)
    ]
    for part in arrived:
        total = total + part.astype(f32)
    return total


def reduce_all(packed):
    core = lax.axis_index("c")
    keep = lax.dynamic_index_in_dim(packed, core, 1, keepdims=False)
    send = lax.dynamic_index_in_dim(packed, 1 - core, 1, keepdims=False)
    arrived = lax.ppermute(send, "c", shifted(2, 1))
    pair = (keep.astype(f32) + arrived.astype(f32)).astype(bf16).reshape(4, 4, ROWS_ALL, LANES)
    one, two = axis_sum(pair[:, :, :ROWS_A], 0, "x"), axis_sum(pair[:, :, ROWS_A:], 1, "y")
    one, two = axis_sum(one.astype(bf16), 0, "y"), axis_sum(two.astype(bf16), 0, "x")
    total = jnp.concatenate([one, two], axis=0).astype(bf16)
    wide = jnp.moveaxis(total[:1152].reshape(24, 4, 12, LANES), 1, 0).reshape(4, 288, LANES)
    tall = jnp.moveaxis(total[1152:1728].reshape(3, 4, 48, LANES), 1, 0).reshape(4, 144, LANES)
    rows = total[1728:1736].reshape(4, 2, LANES)
    total = axis_sum(jnp.concatenate([wide, tall, rows], axis=1), 0, "z")
    wide = total[:288].reshape(24, 2, 6, LANES)
    tall = total[288:432].reshape(3, 2, 24, LANES)
    rows = lax.dynamic_index_in_dim(total[432:], core, 0, keepdims=False)

    def for_core(which):
        a = lax.dynamic_index_in_dim(wide, which, 1, keepdims=False).reshape(144, LANES)
        b = lax.dynamic_index_in_dim(tall, which, 1, keepdims=False).reshape(72, LANES)
        return jnp.concatenate([a, b], axis=0)

    own = for_core(core)
    other = lax.ppermute(for_core(1 - core).astype(bf16), "c", shifted(2, 1)).astype(f32)
    left, right = jnp.where(core == 0, own, other), jnp.where(core == 0, other, own)

    def joined(first, count, height):
        parts = [
            jnp.moveaxis(a[first : first + count * height].reshape(count, height, LANES), 0, 1)
            for a in (left, right)
        ]
        return jnp.concatenate([p.reshape(height, -1) for p in parts], axis=1)

    weights = joined(0, 9, 6), joined(54, 3, 6), joined(72, 12, 6), joined(144, 3, 24)
    vectors, at = [], 0
    for cut in (6, 6, 6, 6, 6, 24, 6, 6, 6):
        vectors.append(rows[at : at + cut])
        at += cut
    return weights, vectors


def layer_norm(total, gain, shift):
    centre = jnp.mean(total, axis=-1, keepdims=True)
    centred = total - centre
    variance = jnp.mean(centred * centred, axis=-1, keepdims=True)
    inverse = lax.rsqrt(variance + EPSILON)
    normed = centred * inverse
    return (normed * gain + shift, normed, inverse)


def norm_back(grad, normed, inverse, gain):
    scaled = grad * gain
    term = (
        scaled
        - jnp.mean(scaled, axis=-1, keepdims=True)
        - normed * jnp.mean(scaled * normed, axis=-1, keepdims=True)
    )
    return (inverse * term, jnp.sum(grad * normed, axis=0), jnp.sum(grad, axis=0))


def segment_rows(lengths, assignment, device, rows):
    count = lengths.shape[0]
    order = jnp.arange(count, dtype=jnp.int32)
    same = assignment[:, None] == assignment[None, :]
    before = order[None, :] < order[:, None]
    offset = jnp.sum(jnp.where(same & before, lengths[None, :], 0), axis=1)
    places = jnp.arange(rows, dtype=jnp.int32)[:, None]
    inside = (
        (assignment[None, :] == device)
        & (places >= offset[None, :])
        & (places < (offset + lengths)[None, :])
    )
    return jnp.sum(jnp.where(inside, order[None, :] + 1, 0), axis=1)


def scores_of(query_heads, key_heads, segment):
    raw = jnp.einsum("qhd,khd->hqk", query_heads, key_heads, preferred_element_type=f32) * SCALE
    allowed = segment[:, None] == segment[None, :]
    return jnp.where(allowed[None], raw, MASK_FILL)


def transpose_product(left, right):
    return jnp.einsum("ti,to->io", left, right, preferred_element_type=f32)


def back_product(grad, weight):
    return jnp.einsum("to,io->ti", grad, weight, preferred_element_type=f32)


def body(
    hidden_in,
    out_cotangent,
    lengths,
    assignment,
    qkv_weight,
    query_bias,
    value_bias,
    out_weight,
    out_bias,
    first_gain,
    first_shift,
    in_weight,
    in_bias,
    back_weight,
    back_bias,
    second_gain,
    second_shift,
):
    rows, width = hidden_in.shape
    heads = HEADS
    head = width // heads
    small = [
        query_bias,
        value_bias,
        out_bias,
        first_gain,
        first_shift,
        in_bias,
        back_bias,
        second_gain,
        second_shift,
    ]
    gathered = gather_all(qkv_weight, out_weight, in_weight, back_weight, small)
    weight_qkv, weight_out, weight_in, weight_back, vectors = unpack(gathered)
    (
        bias_query,
        bias_value,
        bias_out,
        gain_first,
        shift_first,
        bias_in,
        bias_back,
        gain_second,
        shift_second,
    ) = [v.astype(f32) for v in vectors]
    device = ((lax.axis_index("x") * 4 + lax.axis_index("y")) * 4 + lax.axis_index("z")) * 2
    device = device + lax.axis_index("c")
    segment = segment_rows(lengths, assignment, device, rows)
    valid = (segment > 0).astype(f32)[:, None]
    inputs = hidden_in.astype(f32)
    mixed = jnp.dot(hidden_in, weight_qkv, preferred_element_type=f32)
    query_heads = (mixed[:, :width] + bias_query).astype(bf16).reshape(rows, heads, head)
    key_heads = mixed[:, width : 2 * width].astype(bf16).reshape(rows, heads, head)
    value_heads = (mixed[:, 2 * width :] + bias_value).astype(bf16).reshape(rows, heads, head)
    scores = scores_of(query_heads, key_heads, segment)
    top = jnp.max(scores, axis=-1, keepdims=True)
    logsum = top + jnp.log(jnp.sum(jnp.exp(scores - top), axis=-1, keepdims=True))
    probs_low = jnp.exp(scores - logsum).astype(bf16)
    context = jnp.einsum("hqk,khd->qhd", probs_low, value_heads, preferred_element_type=f32)
    context_low = context.reshape(rows, width).astype(bf16)
    attn = jnp.dot(context_low, weight_out, preferred_element_type=f32) + bias_out
    first_norm, normed_first, inverse_first = layer_norm(inputs + attn, gain_first, shift_first)
    first_low = first_norm.astype(bf16)
    pre_act = jnp.dot(first_low, weight_in, preferred_element_type=f32) + bias_in
    act_value, gelu_back = jax.vjp(lambda value: jax.nn.gelu(value, approximate=False), pre_act)
    act_low = act_value.astype(bf16)
    branch = jnp.dot(act_low, weight_back, preferred_element_type=f32) + bias_back
    second_out, normed_second, inverse_second = layer_norm(
        first_norm + branch, gain_second, shift_second
    )
    layer_out = (second_out * valid).astype(bf16)
    grad_out = out_cotangent.astype(f32) * valid
    second_grad, second_gain_term, second_shift_term = norm_back(
        grad_out, normed_second, inverse_second, gain_second
    )
    branch_grad = second_grad.astype(bf16)
    back_weight_term = transpose_product(act_low, branch_grad)
    back_bias_term = jnp.sum(branch_grad.astype(f32), axis=0)
    act_grad = back_product(branch_grad, weight_back)
    pre_grad = gelu_back(act_grad)[0].astype(bf16)
    in_weight_term = transpose_product(first_low, pre_grad)
    in_bias_term = jnp.sum(pre_grad.astype(f32), axis=0)
    first_norm_grad = second_grad + back_product(pre_grad, weight_in)
    first_grad, first_gain_term, first_shift_term = norm_back(
        first_norm_grad, normed_first, inverse_first, gain_first
    )
    attn_grad = first_grad.astype(bf16)
    out_weight_term = transpose_product(context_low, attn_grad)
    out_bias_term = jnp.sum(attn_grad.astype(f32), axis=0)
    context_grad = back_product(attn_grad, weight_out).astype(bf16).reshape(rows, heads, head)
    scores_again = scores_of(query_heads, key_heads, segment)
    probs = jnp.exp(scores_again - logsum)
    probs_again = probs.astype(bf16)
    prob_grad = jnp.einsum("qhd,khd->hqk", context_grad, value_heads, preferred_element_type=f32)
    value_grad = jnp.einsum("hqk,qhd->khd", probs_again, context_grad, preferred_element_type=f32)
    score_grad = (
        probs * (prob_grad - jnp.sum(prob_grad * probs, axis=-1, keepdims=True))
    ).astype(bf16)
    query_grad = jnp.einsum("hqk,khd->qhd", score_grad, key_heads, preferred_element_type=f32)
    key_grad = jnp.einsum("hqk,qhd->khd", score_grad, query_heads, preferred_element_type=f32)
    mixed_grad = jnp.concatenate(
        [
            query_grad.reshape(rows, width) * SCALE,
            key_grad.reshape(rows, width) * SCALE,
            value_grad.reshape(rows, width),
        ],
        axis=1,
    ).astype(bf16)
    qkv_weight_term = transpose_product(hidden_in, mixed_grad)
    mixed_sums = jnp.sum(mixed_grad.astype(f32), axis=0)
    input_grad = (first_grad + back_product(mixed_grad, weight_qkv)).astype(bf16)
    terms = [
        mixed_sums[:width],
        mixed_sums[2 * width :],
        out_bias_term,
        first_gain_term,
        first_shift_term,
        in_bias_term,
        back_bias_term,
        second_gain_term,
        second_shift_term,
    ]
    weights, sums = reduce_all(
        pack(qkv_weight_term, out_weight_term, in_weight_term, back_weight_term, terms)
    )
    return (
        layer_out,
        input_grad,
        weights[0],
        sums[0],
        sums[1],
        weights[1],
        sums[2],
        sums[3],
        sums[4],
        weights[2],
        sums[5],
        weights[3],
        sums[6],
        sums[7],
        sums[8],
    )


def solution(mesh):
    axes = ("x", "y", "z", "c")
    grid = Mesh(mesh.devices.reshape(4, 4, 4, 2), axes)
    two, one, whole = P(axes, None), P(axes), P()
    in_specs = (two, two, whole, whole, two, one, one, two, one, one, one, two, one, two)
    in_specs = in_specs + (one, one, one)
    out_specs = (two, two, two, one, one, two, one, one, one, two, one, two, one, one, one)
    return jax.shard_map(body, mesh=grid, in_specs=in_specs, out_specs=out_specs, check_vma=False)
```

```python
import jax
import jax.numpy as jnp
from jax import lax
from jax.experimental import pallas as pl
from jax.experimental.pallas import tpu as pltpu
from jax.sharding import Mesh, PartitionSpec as P

ROWS = 512
D = 768
FF = 3072
LANES = 128
GROUP = 8
ROWS_ALL = 1744
EPSILON = 1e-05
SCALE = 0.125
MASK_FILL = -1000000000.0
bf16, f32 = jnp.bfloat16, jnp.float32
NAMES = ("bq", "bv", "bo", "g1", "s1", "bi", "bb", "g2", "s2")
CUTS = dict(zip(NAMES, (6, 6, 6, 6, 6, 24, 6, 6, 6)))
AT = dict(zip(NAMES, (0, 6, 12, 18, 24, 30, 54, 60, 66)))
ROW_OF = dict(bq=0, bv=1, bo=2, g1=3, s1=4, bb=5, g2=6, s2=7)
LAST = (((1,), (1,)), ((), ()))
FIRST = (((0,), (0,)), ((), ()))


def shape(dims, kind=f32):
    return jax.ShapeDtypeStruct(dims, kind)


def whole(dims):
    return pl.BlockSpec(dims, lambda *_: (0,) * len(dims), pipeline_mode=pl.Buffered(1))


def kept(dims):
    return pl.BlockSpec(dims, lambda *_: (0,) * len(dims))


def run(kernel, grid, ins, outs, shapes, scratch=(), scalars=0, flops=0, size=0):
    return pl.pallas_call(
        kernel,
        grid_spec=pltpu.PrefetchScalarGridSpec(
            num_scalar_prefetch=scalars,
            grid=grid,
            in_specs=ins,
            out_specs=outs,
            scratch_shapes=scratch,
        ),
        out_shape=shapes,
        compiler_params=pltpu.CompilerParams(vmem_limit_bytes=56 * 1024 * 1024),
        cost_estimate=pl.CostEstimate(flops=flops, bytes_accessed=size, transcendentals=0),
    )


def mul(a, b, dims=(((1,), (0,)), ((), ()))):
    return lax.dot_general(a, b, dims, preferred_element_type=f32)


def shifted(n, step):
    return [(i, (i + step) % n) for i in range(n)]


def thirds(w, half):
    rows = w.shape[0]
    part = w.reshape(rows, 3, 2, 3 * LANES)[:, :, half].reshape(rows, 9, LANES)
    return jnp.moveaxis(part, 1, 0)


def blocks_of(w, half):
    rows, cols = w.shape
    part = w[:, half * (cols // 2) : (half + 1) * (cols // 2)]
    return jnp.moveaxis(part.reshape(rows, -1, LANES), 1, 0)


def gather_all(qkv, out, inw, back, small):
    core = lax.axis_index("c")
    halves = []
    for half in range(2):
        parts = [thirds(qkv, half), blocks_of(out, half), blocks_of(inw, half)]
        halves.append(jnp.concatenate(parts, axis=0).reshape(-1, LANES))
        halves.append(blocks_of(back, half).reshape(-1, LANES))
    row = jnp.concatenate(small + [jnp.zeros((LANES - 72,), bf16)])[None]
    packed = jnp.concatenate(halves + [row, jnp.zeros((15, LANES), bf16)], axis=0)
    near = lax.all_gather(packed, ("z", "c"), tiled=False)
    mine = lax.dynamic_slice_in_dim(near, core * 216, 216, axis=1)
    wide = jnp.moveaxis(mine[:, :144].reshape(GROUP, 24, 6, LANES), 0, 1).reshape(-1, LANES)
    tall = jnp.moveaxis(mine[:, 144:].reshape(GROUP, 3, 24, LANES), 0, 1).reshape(-1, LANES)
    tail = jnp.pad(near[:, 432], ((0, 8), (0, 0)))
    block = jnp.concatenate([wide, tall, tail], axis=0)
    return lax.all_gather(block, ("x", "y", "c"), tiled=False).reshape(16, 2, ROWS_ALL, LANES)


def columns(ref, count, height=48, halves=(0,)):
    rows = ref.shape[0] * height
    parts = [
        ref[:, half, height * j : height * (j + 1), :].reshape(rows, LANES)
        for half in halves
        for j in range(count)
    ]
    return parts[0] if len(parts) == 1 else jnp.concatenate(parts, axis=1)


QKV = [
    pl.BlockSpec((16, 1, 48, LANES), lambda p, t=t: (0, p // 3, 3 * t + p % 3, 0)) for t in range(3)
]
OUT = pl.BlockSpec((16, 2, 144, LANES), lambda *_: (0, 0, 3, 0), pipeline_mode=pl.Buffered(1))
IN = pl.BlockSpec((16, 1, 144, LANES), lambda b: (0, b // 4, 4 + b % 4, 0))
BACK = pl.BlockSpec((2, 2, 576, LANES), lambda b: (b, 0, 2, 0))
SMALL = pl.BlockSpec((16, 1, 16, LANES), lambda *_: (0, 0, 108, 0), pipeline_mode=pl.Buffered(1))
PAIR = pl.BlockSpec((ROWS, LANES), lambda p: (0, p))
WIDE = pl.BlockSpec((ROWS, 384), lambda b: (0, b))


def place_of(cut, shape_, dim):
    at = lax.broadcasted_iota(jnp.int32, shape_, dim)
    owner = (at * (10923 if cut == 6 else 2731)) >> 16
    return owner, at - owner * cut


def spread(rows, name):
    cut = CUTS[name]
    width = cut * 128
    _, place = place_of(cut, (LANES, width), 1)
    pick = lax.broadcasted_iota(jnp.int32, (LANES, width), 0) == place + AT[name]
    every = mul(rows, jnp.where(pick, 1.0, 0.0).astype(bf16))
    owner, _ = place_of(cut, (128, width), 1)
    here = lax.broadcasted_iota(jnp.int32, (128, width), 0) == owner
    return jnp.sum(jnp.where(here, every, 0.0), axis=0, keepdims=True)


def gathered_rows(vectors):
    total = jnp.zeros((128, LANES), f32)
    for name, vector in vectors:
        cut = CUTS[name]
        width = cut * 128
        owner, _ = place_of(cut, (128, width), 1)
        here = lax.broadcasted_iota(jnp.int32, (128, width), 0) == owner
        _, place = place_of(cut, (width, LANES), 0)
        pick = lax.broadcasted_iota(jnp.int32, (width, LANES), 1) == place + AT[name]
        own = jnp.where(here, vector, 0.0).astype(bf16)
        total = total + mul(own, jnp.where(pick, 1.0, 0.0).astype(bf16))
    total = total.reshape(16, 8, LANES)
    return jnp.concatenate([total, jnp.zeros((16, 8, LANES), f32)], axis=1).astype(bf16)


def normalise(total):
    centred = total - jnp.mean(total, axis=-1, keepdims=True)
    inverse = lax.rsqrt(jnp.mean(centred * centred, axis=-1, keepdims=True) + EPSILON)
    return centred * inverse, inverse


def norm_back(grad, normed, inverse, gain):
    scaled = grad * gain
    mean = jnp.mean(scaled, axis=-1, keepdims=True)
    slope = jnp.mean(scaled * normed, axis=-1, keepdims=True)
    return inverse * (scaled - mean - normed * slope)


def column_sum(value):
    return jnp.sum(value, axis=0, keepdims=True)


def head_mask(head):
    lane = lax.broadcasted_iota(jnp.int32, (ROWS, LANES), 1)
    return (lane < 64) if head == 0 else (lane >= 64)


def masked(value, head, factor=1.0):
    return jnp.where(head_mask(head), value.astype(f32) * factor, 0.0).astype(bf16)


def attend_kernel(
    x, sc, sr, wq, wk, wv, wo, sm, q_o, k_o, v_o, lse_o, ctx_o, n1_o, low_o, inv_o, vec_o, bin_o,
    bias, ctx_s,
):
    p = pl.program_id(0)

    @pl.when(p == 0)
    def _():
        bias[...] = jnp.where(sc[...] == sr[...], 0.0, MASK_FILL)
        rows = sm[...].astype(f32)[:, 0, :8, :].reshape(128, LANES).astype(bf16)
        for name, row in ROW_OF.items():
            vec_o[row : row + 1, :] = spread(rows, name)
        bin_o[0:1, :] = spread(rows, "bi")

    weight = jnp.concatenate([columns(w, 1) for w in (wq, wk, wv)], axis=1)
    mixed = mul(x[...], weight)
    lanes = pl.ds(pl.multiple_of(p * LANES, LANES), LANES)
    q = (mixed[:, :LANES] + vec_o[0:1, lanes]).astype(bf16)
    k = mixed[:, LANES : 2 * LANES].astype(bf16)
    value = (mixed[:, 2 * LANES :] + vec_o[1:2, lanes]).astype(bf16)
    q_o[...], k_o[...], v_o[...] = q, k, value
    turned = value.astype(f32).T.astype(bf16)
    parts = []
    for head in range(2):
        scores = mul(k, masked(q, head, SCALE), LAST) + bias[...]
        top = jnp.max(scores, axis=0, keepdims=True)
        raised = jnp.exp(scores - top)
        total = jnp.sum(raised, axis=0, keepdims=True)
        lse_o[0, head : head + 1, :] = top + jnp.log(total)
        probs = (raised * (1.0 / total)).astype(bf16)
        parts.append(mul(turned[64 * head : 64 * (head + 1)], probs))
    context = jnp.concatenate(parts, axis=0).T.astype(bf16)
    ctx_o[...] = context
    ctx_s[:, lanes] = context

    @pl.when(p == 5)
    def _():
        attn = mul(ctx_s[...], columns(wo, 3, halves=(0, 1))) + vec_o[2:3, :]
        normed, inverse = normalise(x[...].astype(f32) + attn)
        n1_o[...], inv_o[...] = normed, inverse
        low_o[...] = (normed * vec_o[3:4, :] + vec_o[4:5, :]).astype(bf16)


def attend(x, seg_col, seg_row, gathered):
    wide, pair = shape((ROWS, D), bf16), PAIR
    return run(
        attend_kernel,
        (6,),
        [whole((ROWS, D)), whole((ROWS, 1)), whole((1, ROWS)), *QKV, OUT, SMALL],
        [pair, pair, pair, pl.BlockSpec((1, 8, ROWS), lambda p: (p, 0, 0)), pair]
        + [kept((ROWS, D)), kept((ROWS, D)), kept((ROWS, 1)), kept((8, D)), kept((8, FF))],
        [wide, wide, wide, shape((6, 8, ROWS)), wide, shape((ROWS, D)), wide, shape((ROWS, 1))]
        + [shape((8, D)), shape((8, FF))],
        [pltpu.VMEM((ROWS, ROWS), f32), pltpu.VMEM((ROWS, D), bf16)],
        flops=6_000_000_000,
        size=12_000_000,
    )(x, seg_col, seg_row, *[gathered] * 5)


def forward_kernel(
    low, n1, sc, cot, vec, bi, wi, wb, act_o, slope_o, out_o, dsec_o, dbr_o, sums_o, acc
):
    b = pl.program_id(0)
    pre = mul(low[...], columns(wi, 3)) + bi[0:1, :]
    share = 0.5 * lax.erf(pre * 0.7071067811865476) + 0.5
    act = (pre * share).astype(bf16)
    act_o[...] = act
    slope_o[...] = (share + pre * (jnp.exp(pre * pre * -0.5) * 0.3989422804014327)).astype(bf16)
    term = mul(act, columns(wb, 3, 192, (0, 1)))

    @pl.when(b == 0)
    def _():
        acc[...] = term

    @pl.when(b > 0)
    def _():
        acc[...] += term

    @pl.when(b == 7)
    def _():
        first = n1[...] * vec[3:4, :] + vec[4:5, :]
        normed, inverse = normalise(first + (acc[...] + vec[5:6, :]))
        valid = jnp.where(sc[...] > 0, 1.0, 0.0)
        out_o[...] = ((normed * vec[6:7, :] + vec[7:8, :]) * valid).astype(bf16)
        grad = cot[...].astype(f32) * valid
        sums_o[0:1, :] = column_sum(grad * normed)
        sums_o[1:2, :] = column_sum(grad)
        second = norm_back(grad, normed, inverse, vec[6:7, :])
        dsec_o[...] = second
        rounded = second.astype(bf16)
        dbr_o[...] = rounded
        sums_o[2:3, :] = column_sum(rounded.astype(f32))


def forward(low, n1, seg_col, cot, vec, bi, gathered):
    deep, wide = shape((ROWS, FF), bf16), shape((ROWS, D), bf16)
    flat = whole((ROWS, D))
    return run(
        forward_kernel,
        (8,),
        [flat, flat, whole((ROWS, 1)), flat, whole((8, D))]
        + [pl.BlockSpec((8, 384), lambda b: (0, b)), IN, BACK],
        [WIDE, WIDE, kept((ROWS, D)), kept((ROWS, D)), kept((ROWS, D)), kept((8, D))],
        [deep, deep, wide, shape((ROWS, D)), wide, shape((8, D))],
        [pltpu.VMEM((ROWS, D), f32)],
        flops=10_000_000_000,
        size=20_000_000,
    )(low, n1, seg_col, cot, vec, bi, gathered, gathered)


def backward_kernel(
    dbr, slope, dsec, n1, inv, vec, wi, wb, wo, dpre_o, bi_o, dfirst_o, dattn_o, dctx_o, sums_o, acc
):
    b = pl.program_id(0)
    dact = mul(dbr[...], columns(wb, 3, 192, (0, 1)), LAST)
    dpre = (dact * slope[...].astype(f32)).astype(bf16)
    dpre_o[...] = dpre
    bi_o[0:1, :] = column_sum(dpre.astype(f32))
    term = mul(dpre, columns(wi, 3), LAST)

    @pl.when(b == 0)
    def _():
        acc[...] = dsec[...] + term

    @pl.when(b > 0)
    def _():
        acc[...] += term

    @pl.when(b == 7)
    def _():
        grad, normed = acc[...], n1[...]
        sums_o[0:1, :] = column_sum(grad * normed)
        sums_o[1:2, :] = column_sum(grad)
        first = norm_back(grad, normed, inv[...], vec[3:4, :])
        dfirst_o[...] = first
        rounded = first.astype(bf16)
        dattn_o[...] = rounded
        sums_o[2:3, :] = column_sum(rounded.astype(f32))
        dctx_o[...] = mul(rounded, columns(wo, 3, halves=(0, 1)), LAST).astype(bf16)


def backward(dbr, slope, dsec, n1, inv, vec, gathered):
    wide, flat = shape((ROWS, D), bf16), whole((ROWS, D))
    return run(
        backward_kernel,
        (8,),
        [flat, WIDE, flat, flat, whole((ROWS, 1)), whole((8, D)), IN, BACK, OUT],
        [WIDE, pl.BlockSpec((8, 384), lambda b: (0, b))]
        + [kept((ROWS, D)), kept((ROWS, D)), kept((ROWS, D)), kept((8, D))],
        [shape((ROWS, FF), bf16), shape((8, FF)), shape((ROWS, D)), wide, wide, shape((8, D))],
        [pltpu.VMEM((ROWS, D), f32)],
        flops=10_000_000_000,
        size=20_000_000,
    )(dbr, slope, dsec, n1, inv, vec, gathered, gathered, gathered)


def attend_back_kernel(
    q, k, v, dctx, lse, sc, sr, dfirst, wq, wk, wv, dq_o, dk_o, dv_o, sums_o, dx_o, bias, acc
):
    p = pl.program_id(0)

    @pl.when(p == 0)
    def _():
        bias[...] = jnp.where(sc[...] == sr[...], 0.0, MASK_FILL)
        acc[...] = dfirst[...]

    key, value = k[...], v[...]
    turned = key.astype(f32).T.astype(bf16)
    dk = jnp.zeros((ROWS, LANES), f32)
    dv = jnp.zeros((ROWS, LANES), f32)
    parts = []
    for head in range(2):
        query = masked(q[...], head, SCALE)
        grad = masked(dctx[...], head)
        probs = jnp.exp(mul(key, query, LAST) + bias[...] - lse[0, head : head + 1, :])
        dprobs = mul(value, grad, LAST)
        dv = dv + mul(probs.astype(bf16), grad)
        dscores = (probs * (dprobs - column_sum(probs * dprobs))).astype(bf16)
        dk = dk + mul(dscores, query)
        parts.append(mul(turned[64 * head : 64 * (head + 1)], dscores))
    dq = (jnp.concatenate(parts, axis=0).T * SCALE).astype(bf16)
    dk, dv = dk.astype(bf16), dv.astype(bf16)
    dq_o[...], dk_o[...], dv_o[...] = dq, dk, dv
    sums_o[0:1, :] = column_sum(dq.astype(f32))
    sums_o[1:2, :] = column_sum(dv.astype(f32))
    weight = jnp.concatenate([columns(w, 1) for w in (wq, wk, wv)], axis=1)
    acc[...] += mul(jnp.concatenate([dq, dk, dv], axis=1), weight, LAST)

    @pl.when(p == 5)
    def _():
        dx_o[...] = acc[...].astype(bf16)


def attend_back(q, k, v, dctx, lse, seg_col, seg_row, dfirst, gathered):
    wide = shape((ROWS, D), bf16)
    return run(
        attend_back_kernel,
        (6,),
        [PAIR, PAIR, PAIR, PAIR, pl.BlockSpec((1, 8, ROWS), lambda p: (p, 0, 0))]
        + [whole((ROWS, 1)), whole((1, ROWS)), whole((ROWS, D)), *QKV],
        [PAIR, PAIR, PAIR, pl.BlockSpec((8, LANES), lambda p: (0, p)), kept((ROWS, D))],
        [wide, wide, wide, shape((8, D)), wide],
        [pltpu.VMEM((ROWS, ROWS), f32), pltpu.VMEM((ROWS, D), f32)],
        flops=10_000_000_000,
        size=12_000_000,
    )(q, k, v, dctx, lse, seg_col, seg_row, dfirst, *[gathered] * 3)


def back_grad_kernel(half, act, dbr, out):
    grad = mul(act[...], dbr[...], FIRST).astype(bf16)
    for at in range(2):
        for j in range(3):
            part = grad[192 * at : 192 * (at + 1), LANES * j : LANES * (j + 1)]
            out[at, 192 * j : 192 * (j + 1), :] = part


def back_grad(half, act, dbr):
    return run(
        back_grad_kernel,
        (8,),
        [
            pl.BlockSpec((ROWS, 384), lambda b, h: (0, b)),
            pl.BlockSpec((ROWS, 384), lambda b, h: (0, h[0])),
        ],
        pl.BlockSpec((2, 576, LANES), lambda b, h: (b, 0, 0)),
        shape((16, 576, LANES), bf16),
        scalars=1,
        flops=1_200_000_000,
        size=6_000_000,
    )(half, act, dbr)


def put(out, at, grad):
    rows = grad.astype(bf16).reshape(16, 48, -1)
    for j in range(rows.shape[2] // LANES):
        out[:, at + 48 * j : at + 48 * (j + 1), :] = rows[:, :, LANES * j : LANES * (j + 1)]


def middle_grad_kernel(half, low, dpre, ctx, dattn, two, bi, one, out):
    turned = low[...].astype(f32).T.astype(bf16)
    for b in range(4):
        put(out, 144 * b, mul(turned, dpre[:, 384 * b : 384 * (b + 1)]))
    put(out, 576, mul(ctx[...], dattn[...], FIRST))
    names = (("g2", two, 0), ("s2", two, 1), ("bb", two, 2), ("bi", bi, 0))
    names = names + (("g1", one, 0), ("s1", one, 1), ("bo", one, 2))
    out[:, 720:736, :] = gathered_rows([(n, ref[i : i + 1, :]) for n, ref, i in names])


def middle_grad(half, low, dpre, ctx, dattn, two, bi, one):
    return run(
        middle_grad_kernel,
        (1,),
        [kept((ROWS, D)), pl.BlockSpec((ROWS, 1536), lambda b, h: (0, h[0])), kept((ROWS, D))]
        + [pl.BlockSpec((ROWS, 384), lambda b, h: (0, h[0]))]
        + [kept((8, D)), kept((8, FF)), kept((8, D))],
        kept((16, 736, LANES)),
        shape((16, 736, LANES), bf16),
        scalars=1,
        flops=1_600_000_000,
        size=8_000_000,
    )(half, low, dpre, ctx, dattn, two, bi, one)


def qkv_grad_kernel(half, x, dq, dk, dv, sums, out):
    turned = x[...].astype(f32).T.astype(bf16)
    for t, ref in enumerate((dq, dk, dv)):
        put(out, 144 * t, mul(turned, ref[...]))
    out[:, 432:448, :] = gathered_rows([("bq", sums[0:1, :]), ("bv", sums[1:2, :])])


def qkv_grad(half, x, dq, dk, dv, sums):
    part = pl.BlockSpec((ROWS, 384), lambda b, h: (0, h[0]))
    return run(
        qkv_grad_kernel,
        (1,),
        [kept((ROWS, D)), part, part, part, kept((8, D))],
        kept((16, 448, LANES)),
        shape((16, 448, LANES), bf16),
        scalars=1,
        flops=1_000_000_000,
        size=5_000_000,
    )(half, x, dq, dk, dv, sums)


def pair_kernel(place, keep, got, *outs):
    rows = keep.shape[1] // 2
    for k in range(4):
        px, py = (place[0] + k) % 4, (place[1] + k) % 4
        for i in range(4):
            at = px * 4 + i
            total = keep[at, :rows, :].astype(f32) + got[at, :rows, :].astype(f32)
            outs[k][i] = total.astype(bf16)
            at = i * 4 + py
            total = keep[at, rows:, :].astype(f32) + got[at, rows:, :].astype(f32)
            outs[4 + k][i] = total.astype(bf16)


def pair_sum(place, keep, got):
    rows = keep.shape[1]
    out = (4, rows // 2, LANES)
    return run(
        pair_kernel,
        (1,),
        [kept((16, rows, LANES))] * 2,
        [kept(out)] * 8,
        [shape(out, bf16)] * 8,
        scalars=1,
        size=16 * rows * LANES * 6,
    )(place, keep, got)


def ring_kernel(place, *refs):
    ins, outs = refs[:8], refs[8:]
    for k in range(4):
        for first, at in ((0, (place[1] + k) % 4), (4, (place[0] + k) % 4)):
            total = ins[first][at].astype(f32)
            for j in range(1, 4):
                total = total + ins[first + j][at].astype(f32)
            outs[first + k][...] = total.astype(bf16)


def ring_sum(place, parts):
    rows = parts[0].shape[1]
    return run(
        ring_kernel,
        (1,),
        [kept((4, rows, LANES))] * 8,
        [kept((rows, LANES))] * 8,
        [shape((rows, LANES), bf16)] * 8,
        scalars=1,
        size=40 * rows * LANES * 2,
    )(place, *parts)


def last_kernel(place, *refs):
    ins, outs = refs[:24], refs[24:]
    sums = []
    for c in range(3):
        halves = []
        for first in (8 * c, 8 * c + 4):
            total = ins[first][...].astype(f32)
            for j in range(1, 4):
                total = total + ins[first + j][...].astype(f32)
            halves.append(total)
        sums.append(jnp.concatenate(halves, axis=0))
    back, middle, qkv = sums
    wide = [qkv[48 * j : 48 * (j + 1)] for j in range(9)]
    wide = wide + [middle[576 + 48 * j : 576 + 48 * (j + 1)] for j in range(3)]
    wide = wide + [middle[48 * j : 48 * (j + 1)] for j in range(12)]
    rows = middle[720:728] + qkv[432:440]
    none = jnp.zeros((4, LANES), f32)
    for z in range(4):
        parts = []
        for block in wide:
            parts = parts + [block[12 * z : 12 * (z + 1)], none]
        for j in range(3):
            parts.append(back[192 * j + 48 * z : 192 * j + 48 * (z + 1)])
        parts = parts + [rows[2 * z : 2 * (z + 1)], jnp.zeros((14, LANES), f32)]
        total = jnp.concatenate(parts, axis=0).astype(bf16)
        for k in range(4):

            @pl.when((place[2] + k) % 4 == z)
            def _():
                outs[k][...] = total


def last_sum(place, parts):
    return run(
        last_kernel,
        (1,),
        [kept(p.shape) for p in parts],
        [kept((544, LANES))] * 4,
        [shape((544, LANES), bf16)] * 4,
        scalars=1,
        size=4_000_000,
    )(place, *parts)


def around(parts, axis):
    return [parts[0]] + [lax.ppermute(parts[k], axis, shifted(4, k)) for k in (1, 3, 2)]


def first_rings(place, keep, send):
    got = lax.ppermute(send, "c", shifted(2, 1))
    parts = pair_sum(place, keep, got)
    return ring_sum(place, around(parts[:4], "x") + around(parts[4:], "y"))


def second_rings(parts):
    return around(parts[:4], "y") + around(parts[4:], "x")


def finish(place, core, parts):
    parts = around(last_sum(place, parts), "z")
    total = sum(p.astype(f32) for p in parts)
    wide = total[:384].reshape(24, 16, LANES)[:, :12].reshape(24, 2, 6, LANES)
    tall = total[384:528].reshape(3, 2, 24, LANES)
    rows = lax.dynamic_index_in_dim(total[528:530], core, 0, keepdims=False)

    def for_core(which):
        a = lax.dynamic_index_in_dim(wide, which, 1, keepdims=False).reshape(144, LANES)
        b = lax.dynamic_index_in_dim(tall, which, 1, keepdims=False).reshape(72, LANES)
        return jnp.concatenate([a, b], axis=0)

    own = for_core(core)
    other = lax.ppermute(for_core(1 - core).astype(bf16), "c", shifted(2, 1)).astype(f32)
    left, right = jnp.where(core == 0, own, other), jnp.where(core == 0, other, own)

    def joined(first, count, height, groups=1):
        parts = [
            jnp.moveaxis(a[first : first + count * height].reshape(count, height, LANES), 0, 1)
            for a in (left, right)
        ]
        parts = [p.reshape(height, groups, -1) for p in parts]
        return jnp.concatenate(parts, axis=2).reshape(height, -1)

    weights = joined(0, 9, 6, 3), joined(54, 3, 6), joined(72, 12, 6), joined(144, 3, 24)
    return weights, {n: rows[AT[n] : AT[n] + CUTS[n]] for n in NAMES}


def segment_rows(lengths, assignment, device, rows):
    count = lengths.shape[0]
    order = jnp.arange(count, dtype=jnp.int32)
    same = assignment[:, None] == assignment[None, :]
    before = order[None, :] < order[:, None]
    offset = jnp.sum(jnp.where(same & before, lengths[None, :], 0), axis=1)
    places = jnp.arange(rows, dtype=jnp.int32)[:, None]
    inside = (
        (assignment[None, :] == device)
        & (places >= offset[None, :])
        & (places < (offset + lengths)[None, :])
    )
    return jnp.sum(jnp.where(inside, order[None, :] + 1, 0), axis=1)


def body(
    hidden_in,
    out_cotangent,
    lengths,
    assignment,
    qkv_weight,
    query_bias,
    value_bias,
    out_weight,
    out_bias,
    first_gain,
    first_shift,
    in_weight,
    in_bias,
    back_weight,
    back_bias,
    second_gain,
    second_shift,
):
    small = [
        query_bias,
        value_bias,
        out_bias,
        first_gain,
        first_shift,
        in_bias,
        back_bias,
        second_gain,
        second_shift,
    ]
    gathered = gather_all(qkv_weight, out_weight, in_weight, back_weight, small)
    px, py, pz, core = (lax.axis_index(a) for a in ("x", "y", "z", "c"))
    place = jnp.stack([px, py, pz]).astype(jnp.int32)
    keep, send = core.reshape(1).astype(jnp.int32), (1 - core).reshape(1).astype(jnp.int32)
    segment = segment_rows(lengths, assignment, ((px * 4 + py) * 4 + pz) * 2 + core, ROWS)
    seg_col, seg_row = segment.reshape(ROWS, 1), segment.reshape(1, ROWS)
    q, k, v, lse, ctx, n1, low, inv, vec, bi = attend(hidden_in, seg_col, seg_row, gathered)
    act, slope, layer_out, dsec, dbr, two = forward(
        low, n1, seg_col, out_cotangent, vec, bi, gathered
    )
    back = first_rings(place, back_grad(keep, act, dbr), back_grad(send, act, dbr))
    dpre, dbi, dfirst, dattn, dctx, one = backward(dbr, slope, dsec, n1, inv, vec, gathered)
    middle = first_rings(
        place,
        middle_grad(keep, low, dpre, ctx, dattn, two, dbi, one),
        middle_grad(send, low, dpre, ctx, dattn, two, dbi, one),
    )
    dq, dk, dv, sums, input_grad = attend_back(
        q, k, v, dctx, lse, seg_col, seg_row, dfirst, gathered
    )
    qkv = first_rings(
        place, qkv_grad(keep, hidden_in, dq, dk, dv, sums), qkv_grad(send, hidden_in, dq, dk, dv, sums)
    )
    parts = [p for c in (back, middle, qkv) for p in second_rings(c)]
    weights, s = finish(place, core, parts)
    return (
        layer_out,
        input_grad,
        weights[0],
        s["bq"],
        s["bv"],
        weights[1],
        s["bo"],
        s["g1"],
        s["s1"],
        weights[2],
        s["bi"],
        weights[3],
        s["bb"],
        s["g2"],
        s["s2"],
    )


def solution(mesh):
    axes = ("x", "y", "z", "c")
    grid = Mesh(mesh.devices.reshape(4, 4, 4, 2), axes)
    two, one, every = P(axes, None), P(axes), P()
    in_specs = (two, two, every, every, two, one, one, two, one, one, one, two, one, two)
    in_specs = in_specs + (one, one, one)
    out_specs = (two, two, two, one, one, two, one, one, one, two, one, two, one, one, one)
    return jax.shard_map(body, mesh=grid, in_specs=in_specs, out_specs=out_specs, check_vma=False)
```

```python
import jax
import jax.numpy as jnp
from jax import lax
from jax.experimental import pallas as pl
from jax.experimental.pallas import tpu as pltpu
from jax.sharding import Mesh, PartitionSpec as P

ROWS = 512
D = 768
FF = 3072
LANES = 128
GROUP = 8
ROWS_ALL = 1744
EPSILON = 1e-05
SCALE = 0.125
MASK_FILL = -1000000000.0
bf16, f32 = jnp.bfloat16, jnp.float32
NAMES = ("bq", "bv", "bo", "g1", "s1", "bi", "bb", "g2", "s2")
CUTS = dict(zip(NAMES, (6, 6, 6, 6, 6, 24, 6, 6, 6)))
AT = dict(zip(NAMES, (0, 6, 12, 18, 24, 30, 54, 60, 66)))
ROW_OF = dict(bq=0, bv=1, bo=2, g1=3, s1=4, bb=5, g2=6, s2=7)
LAST = (((1,), (1,)), ((), ()))
FIRST = (((0,), (0,)), ((), ()))


def shape(dims, kind=f32):
    return jax.ShapeDtypeStruct(dims, kind)


def whole(dims):
    return pl.BlockSpec(dims, lambda *_: (0,) * len(dims), pipeline_mode=pl.Buffered(1))


def kept(dims):
    return pl.BlockSpec(dims, lambda *_: (0,) * len(dims))


def run(kernel, grid, ins, outs, shapes, scratch=(), scalars=0, flops=0, size=0, alias=None):
    return pl.pallas_call(
        kernel,
        grid_spec=pltpu.PrefetchScalarGridSpec(
            num_scalar_prefetch=scalars,
            grid=grid,
            in_specs=ins,
            out_specs=outs,
            scratch_shapes=scratch,
        ),
        out_shape=shapes,
        input_output_aliases=alias or {},
        compiler_params=pltpu.CompilerParams(vmem_limit_bytes=63 * 1024 * 1024),
        cost_estimate=pl.CostEstimate(flops=flops, bytes_accessed=size, transcendentals=0),
    )


def mul(a, b, dims=(((1,), (0,)), ((), ()))):
    return lax.dot_general(a, b, dims, preferred_element_type=f32)


def shifted(n, step):
    return [(i, (i + step) % n) for i in range(n)]


def thirds(w, half):
    rows = w.shape[0]
    part = w.reshape(rows, 3, 2, 3 * LANES)[:, :, half].reshape(rows, 9, LANES)
    return jnp.moveaxis(part, 1, 0)


def blocks_of(w, half):
    rows, cols = w.shape
    part = w[:, half * (cols // 2) : (half + 1) * (cols // 2)]
    return jnp.moveaxis(part.reshape(rows, -1, LANES), 1, 0)


def gather_all(qkv, out, inw, back, small):
    core = lax.axis_index("c")
    halves = []
    for half in range(2):
        parts = [thirds(qkv, half), blocks_of(out, half), blocks_of(inw, half)]
        halves.append(jnp.concatenate(parts, axis=0).reshape(-1, LANES))
        halves.append(blocks_of(back, half).reshape(-1, LANES))
    row = jnp.concatenate(small + [jnp.zeros((LANES - 72,), bf16)])[None]
    packed = jnp.concatenate(halves + [row, jnp.zeros((15, LANES), bf16)], axis=0)
    near = lax.all_gather(packed, ("z", "c"), tiled=False)
    mine = lax.dynamic_slice_in_dim(near, core * 216, 216, axis=1)
    wide = jnp.moveaxis(mine[:, :144].reshape(GROUP, 24, 6, LANES), 0, 1).reshape(-1, LANES)
    tall = jnp.moveaxis(mine[:, 144:].reshape(GROUP, 3, 24, LANES), 0, 1).reshape(-1, LANES)
    tail = jnp.pad(near[:, 432], ((0, 8), (0, 0)))
    block = jnp.concatenate([wide, tall, tail], axis=0)
    return lax.all_gather(block, ("x", "y", "c"), tiled=False).reshape(16, 2, ROWS_ALL, LANES)


def columns(ref, count, height=48, halves=(0,)):
    rows = ref.shape[0] * height
    parts = [
        ref[:, half, height * j : height * (j + 1), :].reshape(rows, LANES)
        for half in halves
        for j in range(count)
    ]
    return parts[0] if len(parts) == 1 else jnp.concatenate(parts, axis=1)


QKV = [
    pl.BlockSpec((16, 1, 48, LANES), lambda p, t=t: (0, p // 3, 3 * t + p % 3, 0)) for t in range(3)
]
OUT = pl.BlockSpec((16, 2, 144, LANES), lambda *_: (0, 0, 3, 0), pipeline_mode=pl.Buffered(1))
IN = pl.BlockSpec((16, 1, 144, LANES), lambda b: (0, b // 4, 4 + b % 4, 0))
BACK = pl.BlockSpec((2, 2, 576, LANES), lambda b: (b, 0, 2, 0))
SMALL = pl.BlockSpec((16, 1, 16, LANES), lambda *_: (0, 0, 108, 0), pipeline_mode=pl.Buffered(1))
PAIR = pl.BlockSpec((ROWS, LANES), lambda p: (0, p))
WIDE = pl.BlockSpec((ROWS, 384), lambda b: (0, b))


def place_of(cut, shape_, dim):
    at = lax.broadcasted_iota(jnp.int32, shape_, dim)
    owner = (at * (10923 if cut == 6 else 2731)) >> 16
    return owner, at - owner * cut


def spread(rows, name):
    cut = CUTS[name]
    width = cut * 128
    _, place = place_of(cut, (LANES, width), 1)
    pick = lax.broadcasted_iota(jnp.int32, (LANES, width), 0) == place + AT[name]
    every = mul(rows, jnp.where(pick, 1.0, 0.0).astype(bf16))
    owner, _ = place_of(cut, (128, width), 1)
    here = lax.broadcasted_iota(jnp.int32, (128, width), 0) == owner
    return jnp.sum(jnp.where(here, every, 0.0), axis=0, keepdims=True)


def gathered_rows(vectors):
    total = jnp.zeros((128, LANES), f32)
    for name, vector in vectors:
        cut = CUTS[name]
        width = cut * 128
        owner, _ = place_of(cut, (128, width), 1)
        here = lax.broadcasted_iota(jnp.int32, (128, width), 0) == owner
        _, place = place_of(cut, (width, LANES), 0)
        pick = lax.broadcasted_iota(jnp.int32, (width, LANES), 1) == place + AT[name]
        own = jnp.where(here, vector, 0.0).astype(bf16)
        total = total + mul(own, jnp.where(pick, 1.0, 0.0).astype(bf16))
    total = total.reshape(16, 8, LANES)
    return jnp.concatenate([total, jnp.zeros((16, 8, LANES), f32)], axis=1).astype(bf16)


def normalise(total):
    centred = total - jnp.mean(total, axis=-1, keepdims=True)
    inverse = lax.rsqrt(jnp.mean(centred * centred, axis=-1, keepdims=True) + EPSILON)
    return centred * inverse, inverse


def norm_back(grad, normed, inverse, gain):
    scaled = grad * gain
    mean = jnp.mean(scaled, axis=-1, keepdims=True)
    slope = jnp.mean(scaled * normed, axis=-1, keepdims=True)
    return inverse * (scaled - mean - normed * slope)


def column_sum(value):
    return jnp.sum(value, axis=0, keepdims=True)


def head_mask(head):
    lane = lax.broadcasted_iota(jnp.int32, (ROWS, LANES), 1)
    return (lane < 64) if head == 0 else (lane >= 64)


def masked(value, head, factor=1.0):
    return jnp.where(head_mask(head), value.astype(f32) * factor, 0.0).astype(bf16)


def attend_kernel(
    x, sc, sr, wq, wk, wv, wo, sm, q_o, k_o, v_o, lse_o, ctx_o, n1_o, low_o, turn_o, inv_o, vec_o,
    bin_o, bias, ctx_s,
):
    p = pl.program_id(0)

    @pl.when(p == 0)
    def _():
        bias[...] = jnp.where(sc[...] == sr[...], 0.0, MASK_FILL)
        rows = sm[...].astype(f32)[:, 0, :8, :].reshape(128, LANES).astype(bf16)
        for name, row in ROW_OF.items():
            vec_o[row : row + 1, :] = spread(rows, name)
        bin_o[0:1, :] = spread(rows, "bi")

    weight = jnp.concatenate([columns(w, 1) for w in (wq, wk, wv)], axis=1)
    mixed = mul(x[...], weight)
    lanes = pl.ds(pl.multiple_of(p * LANES, LANES), LANES)
    q = (mixed[:, :LANES] + vec_o[0:1, lanes]).astype(bf16)
    k = mixed[:, LANES : 2 * LANES].astype(bf16)
    value = (mixed[:, 2 * LANES :] + vec_o[1:2, lanes]).astype(bf16)
    q_o[...], k_o[...], v_o[...] = q, k, value
    turned = value.astype(f32).T.astype(bf16)
    parts = []
    for head in range(2):
        scores = mul(k, masked(q, head, SCALE), LAST) + bias[...]
        top = jnp.max(scores, axis=0, keepdims=True)
        raised = jnp.exp(scores - top)
        total = jnp.sum(raised, axis=0, keepdims=True)
        lse_o[0, head : head + 1, :] = top + jnp.log(total)
        probs = (raised * (1.0 / total)).astype(bf16)
        parts.append(mul(turned[64 * head : 64 * (head + 1)], probs))
    context = jnp.concatenate(parts, axis=0)
    ctx_o[...] = context.astype(bf16)
    ctx_s[:, lanes] = context.T.astype(bf16)

    @pl.when(p == 5)
    def _():
        attn = mul(ctx_s[...], columns(wo, 3, halves=(0, 1))) + vec_o[2:3, :]
        normed, inverse = normalise(x[...].astype(f32) + attn)
        n1_o[...], inv_o[...] = normed, inverse
        first = normed * vec_o[3:4, :] + vec_o[4:5, :]
        low_o[...], turn_o[...] = first.astype(bf16), first.T.astype(bf16)


def attend(x, seg_col, seg_row, gathered):
    wide, tall, pair = shape((ROWS, D), bf16), shape((D, ROWS), bf16), PAIR
    return run(
        attend_kernel,
        (6,),
        [whole((ROWS, D)), whole((ROWS, 1)), whole((1, ROWS)), *QKV, OUT, SMALL],
        [pair, pair, pair, pl.BlockSpec((1, 8, ROWS), lambda p: (p, 0, 0))]
        + [pl.BlockSpec((LANES, ROWS), lambda p: (p, 0)), kept((ROWS, D)), kept((ROWS, D))]
        + [kept((D, ROWS)), kept((ROWS, 1)), kept((8, D)), kept((8, FF))],
        [wide, wide, wide, shape((6, 8, ROWS)), tall, shape((ROWS, D)), wide, tall]
        + [shape((ROWS, 1)), shape((8, D)), shape((8, FF))],
        [pltpu.VMEM((ROWS, ROWS), f32), pltpu.VMEM((ROWS, D), bf16)],
        flops=6_000_000_000,
        size=12_000_000,
    )(x, seg_col, seg_row, *[gathered] * 5)


def forward_kernel(
    low, n1, sc, cot, vec, bi, wi, wb, act_o, slope_o, out_o, dsec_o, dbr_o, sums_o, acc
):
    b = pl.program_id(0)
    pre = mul(low[...], columns(wi, 3)) + bi[0:1, :]
    share = 0.5 * lax.erf(pre * 0.7071067811865476) + 0.5
    act = pre * share
    act_o[...] = act.T.astype(bf16)
    act = act.astype(bf16)
    slope_o[...] = (share + pre * (jnp.exp(pre * pre * -0.5) * 0.3989422804014327)).astype(bf16)
    term = mul(act, columns(wb, 3, 192, (0, 1)))

    @pl.when(b == 0)
    def _():
        acc[...] = term

    @pl.when(b > 0)
    def _():
        acc[...] += term

    @pl.when(b == 7)
    def _():
        first = n1[...] * vec[3:4, :] + vec[4:5, :]
        normed, inverse = normalise(first + (acc[...] + vec[5:6, :]))
        valid = jnp.where(sc[...] > 0, 1.0, 0.0)
        out_o[...] = ((normed * vec[6:7, :] + vec[7:8, :]) * valid).astype(bf16)
        grad = cot[...].astype(f32) * valid
        sums_o[0:1, :] = column_sum(grad * normed)
        sums_o[1:2, :] = column_sum(grad)
        second = norm_back(grad, normed, inverse, vec[6:7, :])
        dsec_o[...] = second
        rounded = second.astype(bf16)
        dbr_o[...] = rounded
        sums_o[2:3, :] = column_sum(rounded.astype(f32))


def forward(low, n1, seg_col, cot, vec, bi, gathered):
    deep, wide = shape((ROWS, FF), bf16), shape((ROWS, D), bf16)
    flat = whole((ROWS, D))
    return run(
        forward_kernel,
        (8,),
        [flat, flat, whole((ROWS, 1)), flat, whole((8, D))]
        + [pl.BlockSpec((8, 384), lambda b: (0, b)), IN, BACK],
        [pl.BlockSpec((384, ROWS), lambda b: (b, 0)), WIDE]
        + [kept((ROWS, D)), kept((ROWS, D)), kept((ROWS, D)), kept((8, D))],
        [shape((FF, ROWS), bf16), deep, wide, shape((ROWS, D)), wide, shape((8, D))],
        [pltpu.VMEM((ROWS, D), f32)],
        flops=10_000_000_000,
        size=20_000_000,
    )(low, n1, seg_col, cot, vec, bi, gathered, gathered)


def backward_one_kernel(dbr, slope, dsec, wi, wb, dpre_o, bi_o, acc):
    b = pl.program_id(0)
    dact = mul(dbr[...], columns(wb, 3, 192, (0, 1)), LAST)
    dpre = (dact * slope[...].astype(f32)).astype(bf16)
    dpre_o[...] = dpre
    bi_o[0:1, :] = column_sum(dpre.astype(f32))
    term = mul(dpre, columns(wi, 3), LAST)

    @pl.when(b == 0)
    def _():
        acc[...] = dsec[...] + term

    @pl.when(b > 0)
    def _():
        acc[...] += term


def backward_two_kernel(
    dbr, slope, dsec, wi, wb, wo, n1, inv, vec, dpre_in, bi_in, dpre_o, bi_o, dfirst_o, dattn_o,
    dctx_o, sums_o, acc,
):
    backward_one_kernel(dbr, slope, dsec, wi, wb, dpre_o, bi_o, acc)

    @pl.when(pl.program_id(0) == 3)
    def _():
        grad, normed = acc[...], n1[...]
        sums_o[0:1, :] = column_sum(grad * normed)
        sums_o[1:2, :] = column_sum(grad)
        first = norm_back(grad, normed, inv[...], vec[3:4, :])
        dfirst_o[...] = first
        rounded = first.astype(bf16)
        dattn_o[...] = rounded
        sums_o[2:3, :] = column_sum(rounded.astype(f32))
        dctx_o[...] = mul(rounded, columns(wo, 3, halves=(0, 1)), LAST).astype(bf16)


def backward_specs(half):
    ins = [
        whole((ROWS, D)),
        pl.BlockSpec((ROWS, 384), lambda b: (0, 4 * half + b)),
        whole((ROWS, D)),
        pl.BlockSpec((16, 1, 144, LANES), lambda b: (0, half, 4 + b, 0)),
        pl.BlockSpec((2, 2, 576, LANES), lambda b: (4 * half + b, 0, 2, 0)),
    ]
    outs = [
        pl.BlockSpec((ROWS, 384), lambda b: (0, 4 * half + b)),
        pl.BlockSpec((8, 384), lambda b: (0, 4 * half + b)),
    ]
    return ins, outs, [shape((ROWS, FF), bf16), shape((8, FF))]


def backward_one(dbr, slope, dsec, gathered):
    ins, outs, shapes = backward_specs(0)
    return run(
        backward_one_kernel,
        (4,),
        ins,
        outs + [kept((ROWS, D))],
        shapes + [shape((ROWS, D))],
        flops=5_000_000_000,
        size=10_000_000,
    )(dbr, slope, dsec, gathered, gathered)


def backward_two(dbr, slope, acc, n1, inv, vec, dpre, bi, gathered):
    wide, flat = shape((ROWS, D), bf16), whole((ROWS, D))
    ins, outs, shapes = backward_specs(1)
    anywhere = pl.BlockSpec(memory_space=pl.ANY)
    return run(
        backward_two_kernel,
        (4,),
        ins + [OUT, flat, whole((ROWS, 1)), whole((8, D)), anywhere, anywhere],
        outs + [kept((ROWS, D)), kept((ROWS, D)), kept((ROWS, D)), kept((8, D))],
        shapes + [shape((ROWS, D)), wide, wide, shape((8, D))],
        [pltpu.VMEM((ROWS, D), f32)],
        flops=6_000_000_000,
        size=10_000_000,
        alias={9: 0, 10: 1},
    )(dbr, slope, acc, gathered, gathered, gathered, n1, inv, vec, dpre, bi)


def attend_back_kernel(
    q, k, v, dctx, lse, sc, sr, dfirst, wq, wk, wv, mixed_o, sums_o, dx_o, bias, acc
):
    p = pl.program_id(0)

    @pl.when(p == 0)
    def _():
        bias[...] = jnp.where(sc[...] == sr[...], 0.0, MASK_FILL)
        acc[...] = dfirst[...]

    key, value = k[...], v[...]
    turned = key.astype(f32).T.astype(bf16)
    dk = jnp.zeros((ROWS, LANES), f32)
    dv = jnp.zeros((ROWS, LANES), f32)
    parts = []
    for head in range(2):
        query = masked(q[...], head, SCALE)
        grad = masked(dctx[...], head)
        probs = jnp.exp(mul(key, query, LAST) + bias[...] - lse[0, head : head + 1, :])
        dprobs = mul(value, grad, LAST)
        dv = dv + mul(probs.astype(bf16), grad)
        dscores = (probs * (dprobs - column_sum(probs * dprobs))).astype(bf16)
        dk = dk + mul(dscores, query)
        parts.append(mul(turned[64 * head : 64 * (head + 1)], dscores))
    dq = (jnp.concatenate(parts, axis=0).T * SCALE).astype(bf16)
    dk, dv = dk.astype(bf16), dv.astype(bf16)
    mixed_o[0], mixed_o[1], mixed_o[2] = dq, dk, dv
    sums_o[0:1, :] = column_sum(dq.astype(f32))
    sums_o[1:2, :] = column_sum(dv.astype(f32))
    weight = jnp.concatenate([columns(w, 1) for w in (wq, wk, wv)], axis=1)
    acc[...] += mul(jnp.concatenate([dq, dk, dv], axis=1), weight, LAST)

    @pl.when(p == 2)
    def _():
        dx_o[...] = acc[...].astype(dx_o.dtype)


def attend_back(half, q, k, v, dctx, lse, seg_col, seg_row, dfirst, gathered):
    pair = pl.BlockSpec((ROWS, LANES), lambda p: (0, 3 * half + p))
    weights = [
        pl.BlockSpec((16, 1, 48, LANES), lambda p, t=t: (0, half, 3 * t + p, 0)) for t in range(3)
    ]
    return run(
        attend_back_kernel,
        (3,),
        [pair, pair, pair, pair, pl.BlockSpec((1, 8, ROWS), lambda p: (3 * half + p, 0, 0))]
        + [whole((ROWS, 1)), whole((1, ROWS)), whole((ROWS, D)), *weights],
        [pl.BlockSpec((3, ROWS, LANES), lambda p: (0, 0, p))]
        + [pl.BlockSpec((8, LANES), lambda p: (0, p)), kept((ROWS, D))],
        [shape((3, ROWS, 384), bf16), shape((8, 384)), shape((ROWS, D), (f32, bf16)[half])],
        [pltpu.VMEM((ROWS, ROWS), f32), pltpu.VMEM((ROWS, D), f32)],
        flops=6_000_000_000,
        size=8_000_000,
    )(q, k, v, dctx, lse, seg_col, seg_row, dfirst, *[gathered] * 3)


def parts_of(rows):
    out = (4, rows // 2, LANES)
    return dict(outs=[kept(out)] * 8, shapes=[shape(out, bf16)] * 8)


def hand_out(place, total, outs):
    rows = total.shape[1] // 2
    for k in range(4):
        px, py = (place[0] + k) % 4, (place[1] + k) % 4
        for i in range(4):
            outs[k][i] = total[px * 4 + i, :rows, :]
            outs[4 + k][i] = total[i * 4 + py, rows:, :]


def put(total, at, grad):
    rows = grad.astype(bf16).reshape(16, 48, -1)
    for j in range(rows.shape[2] // LANES):
        total[:, pl.ds(at + 48 * j, 48), :] = rows[:, :, LANES * j : LANES * (j + 1)]


def back_grad_kernel(place, act, act_2, dbr, dbr_2, *refs):
    outs, total = refs[:8], refs[8]
    b = pl.program_id(0)
    grad = (mul(act[...], dbr[...]) + mul(act_2[...], dbr_2[...])).astype(bf16)
    for at in range(2):
        for j in range(3):
            part = grad[192 * at : 192 * (at + 1), LANES * j : LANES * (j + 1)]
            total[2 * b + at, 192 * j : 192 * (j + 1), :] = part

    @pl.when(b == 7)
    def _():
        hand_out(place, total, outs)


def back_grad(place, act, act_2, dbr, dbr_2):
    tall = pl.BlockSpec((384, ROWS), lambda b, p: (b, 0))
    half = pl.BlockSpec((ROWS, 384), lambda b, p: (0, p[3]))
    return run(
        back_grad_kernel,
        (8,),
        [tall, tall, half, half],
        scratch=[pltpu.VMEM((16, 576, LANES), bf16)],
        scalars=1,
        flops=2_400_000_000,
        size=10_000_000,
        **parts_of(576),
    )(place, act, act_2, dbr, dbr_2)


def middle_grad_kernel(
    place, low, low_2, dpre, dpre_2, ctx, ctx_2, dattn, dattn_2, two, bi, one, *refs
):
    outs, total = refs[:8], refs[8]
    b = pl.program_id(0)

    @pl.when(b < 4)
    def _():
        grad = mul(low[...], dpre[...]) + mul(low_2[...], dpre_2[...])
        put(total, pl.multiple_of(144 * b, 16), grad)

    @pl.when(b == 4)
    def _():
        put(total, 576, mul(ctx[...], dattn[...]) + mul(ctx_2[...], dattn_2[...]))
        names = (("g2", two, 0), ("s2", two, 1), ("bb", two, 2), ("bi", bi, 0))
        names = names + (("g1", one, 0), ("s1", one, 1), ("bo", one, 2))
        total[:, 720:736, :] = gathered_rows([(n, ref[i : i + 1, :]) for n, ref, i in names])
        hand_out(place, total, outs)


def middle_grad(place, low, low_2, dpre, dpre_2, ctx, ctx_2, dattn, dattn_2, two, bi, one):
    tall = whole((D, ROWS))
    quarter = pl.BlockSpec((ROWS, 384), lambda b, p: (0, 4 * p[3] + jnp.minimum(b, 3)))
    half = pl.BlockSpec((ROWS, 384), lambda b, p: (0, p[3]))
    return run(
        middle_grad_kernel,
        (5,),
        [tall, tall, quarter, quarter, tall, tall, half, half]
        + [whole((8, D)), whole((8, FF)), whole((8, D))],
        scratch=[pltpu.VMEM((16, 736, LANES), bf16)],
        scalars=1,
        flops=3_200_000_000,
        size=12_000_000,
        **parts_of(736),
    )(place, low, low_2, dpre, dpre_2, ctx, ctx_2, dattn, dattn_2, two, bi, one)


def qkv_grad_kernel(place, x, x_2, left, left_2, right, right_2, sums_l, sums_r, *refs):
    outs, total = refs[:8], refs[8]
    for core, own, other in ((0, left, left_2), (1, right, right_2)):

        @pl.when(place[3] == core)
        def _():
            for t in range(3):
                put(total, 144 * t, mul(x[...], own[t]) + mul(x_2[...], other[t]))

    sums = [jnp.concatenate([sums_l[i : i + 1, :], sums_r[i : i + 1, :]], axis=1) for i in (0, 1)]
    total[:, 432:448, :] = gathered_rows([("bq", sums[0]), ("bv", sums[1])])
    hand_out(place, total, outs)


def qkv_grad(place, x, x_2, left, left_2, right, right_2, sums_l, sums_r):
    half = kept((3, ROWS, 384))
    return run(
        qkv_grad_kernel,
        (1,),
        [kept((D, ROWS)), kept((D, ROWS)), half, half, half, half, kept((8, 384)), kept((8, 384))],
        scratch=[pltpu.VMEM((16, 448, LANES), bf16)],
        scalars=1,
        flops=1_800_000_000,
        size=7_000_000,
        **parts_of(448),
    )(place, x, x_2, left, left_2, right, right_2, sums_l, sums_r)


def ring_kernel(place, *refs):
    outs = refs[-8:]
    refs, at = refs[:-8], 0
    while refs:
        ins, refs = refs[:8], refs[8:]
        if len(ins[0].shape) == 2:
            rows = ins[0].shape[0]
            for k in range(8):
                outs[k][at : at + rows, :] = ins[k][...]
            at += rows
            continue
        rows = ins[0].shape[1]
        for k in range(4):
            for first, here in ((0, (place[1] + k) % 4), (4, (place[0] + k) % 4)):
                total = ins[first][here].astype(f32)
                for j in range(1, 4):
                    total = total + ins[first + j][here].astype(f32)
                outs[first + k][at : at + rows, :] = total.astype(bf16)
        at += rows


def ring_sum(place, parts):
    rows = sum(p.shape[-2] for p in parts[::8])
    return run(
        ring_kernel,
        (1,),
        [kept(p.shape) for p in parts],
        [kept((rows, LANES))] * 8,
        [shape((rows, LANES), bf16)] * 8,
        scalars=1,
        size=40 * rows * LANES * 2,
    )(place, *parts)


def last_kernel(place, *refs):
    ins, outs = refs[:8], refs[8:]
    halves = []
    for first in (0, 4):
        total = ins[first][...].astype(f32)
        for j in range(1, 4):
            total = total + ins[first + j][...].astype(f32)
        halves.append(total)
    back = jnp.concatenate([part[:288] for part in halves], axis=0)
    middle = jnp.concatenate([part[288:656] for part in halves], axis=0)
    qkv = jnp.concatenate([part[656:] for part in halves], axis=0)
    wide = [qkv[48 * j : 48 * (j + 1)] for j in range(9)]
    wide = wide + [middle[576 + 48 * j : 576 + 48 * (j + 1)] for j in range(3)]
    wide = wide + [middle[48 * j : 48 * (j + 1)] for j in range(12)]
    rows = middle[720:728] + qkv[432:440]
    none = jnp.zeros((4, LANES), f32)
    for z in range(4):
        parts = []
        for block in wide:
            parts = parts + [block[12 * z : 12 * (z + 1)], none]
        for j in range(3):
            parts.append(back[192 * j + 48 * z : 192 * j + 48 * (z + 1)])
        parts = parts + [rows[2 * z : 2 * (z + 1)], jnp.zeros((14, LANES), f32)]
        total = jnp.concatenate(parts, axis=0).astype(bf16)
        for k in range(4):

            @pl.when((place[2] + k) % 4 == z)
            def _():
                outs[k][...] = total


def last_sum(place, parts):
    return run(
        last_kernel,
        (1,),
        [kept(p.shape) for p in parts],
        [kept((544, LANES))] * 4,
        [shape((544, LANES), bf16)] * 4,
        scalars=1,
        size=4_000_000,
    )(place, *parts)


def around(parts, axis):
    return [parts[0]] + [lax.ppermute(parts[k], axis, shifted(4, k)) for k in (1, 3, 2)]


def to_near(parts):
    steps = ((1, 1, "x"), (3, 3, "x"), (5, 1, "y"), (7, 3, "y"))
    return [lax.ppermute(parts[i], axis, shifted(4, k)) for i, k, axis in steps]


def to_far(parts):
    return [lax.ppermute(parts[i], axis, shifted(4, 2)) for i, axis in ((2, "x"), (6, "y"))]


def arrived(parts, near, far):
    return [parts[0], *near[:2], far[0], parts[4], *near[2:], far[1]]


def second_rings(parts):
    return around(parts[:4], "y") + around(parts[4:], "x")


def swap(value):
    return lax.ppermute(value, "c", shifted(2, 1))


def together(*values):
    flat, tree = jax.tree.flatten(values)
    return jax.tree.unflatten(tree, lax.optimization_barrier(tuple(flat)))


def finish(place, core, parts):
    parts = around(last_sum(place, parts), "z")
    total = sum(p.astype(f32) for p in parts)
    wide = total[:384].reshape(24, 16, LANES)[:, :12].reshape(24, 2, 6, LANES)
    tall = total[384:528].reshape(3, 2, 24, LANES)

    def for_core(which):
        a = lax.dynamic_index_in_dim(wide, which, 1, keepdims=False).reshape(144, LANES)
        b = lax.dynamic_index_in_dim(tall, which, 1, keepdims=False).reshape(72, LANES)
        row = lax.dynamic_index_in_dim(total[528:530], which, 0)
        return jnp.concatenate([a, b, row], axis=0)

    own = for_core(core)
    other = lax.ppermute(for_core(1 - core).astype(bf16), "c", shifted(2, 1)).astype(f32)
    rows = own[216] + other[216]
    left, right = jnp.where(core == 0, own, other), jnp.where(core == 0, other, own)

    def joined(first, count, height, groups=1):
        parts = [
            jnp.moveaxis(a[first : first + count * height].reshape(count, height, LANES), 0, 1)
            for a in (left, right)
        ]
        parts = [p.reshape(height, groups, -1) for p in parts]
        return jnp.concatenate(parts, axis=2).reshape(height, -1)

    weights = joined(0, 9, 6, 3), joined(54, 3, 6), joined(72, 12, 6), joined(144, 3, 24)
    return weights, {n: rows[AT[n] : AT[n] + CUTS[n]] for n in NAMES}


def segment_rows(lengths, assignment, device, rows):
    count = lengths.shape[0]
    order = jnp.arange(count, dtype=jnp.int32)
    same = assignment[:, None] == assignment[None, :]
    before = order[None, :] < order[:, None]
    offset = jnp.sum(jnp.where(same & before, lengths[None, :], 0), axis=1)
    places = jnp.arange(rows, dtype=jnp.int32)[:, None]
    inside = (
        (assignment[None, :] == device)
        & (places >= offset[None, :])
        & (places < (offset + lengths)[None, :])
    )
    return jnp.sum(jnp.where(inside, order[None, :] + 1, 0), axis=1)


def body(
    hidden_in,
    out_cotangent,
    lengths,
    assignment,
    qkv_weight,
    query_bias,
    value_bias,
    out_weight,
    out_bias,
    first_gain,
    first_shift,
    in_weight,
    in_bias,
    back_weight,
    back_bias,
    second_gain,
    second_shift,
):
    small = [
        query_bias,
        value_bias,
        out_bias,
        first_gain,
        first_shift,
        in_bias,
        back_bias,
        second_gain,
        second_shift,
    ]
    gathered = gather_all(qkv_weight, out_weight, in_weight, back_weight, small)
    px, py, pz, core = (lax.axis_index(a) for a in ("x", "y", "z", "c"))
    place = jnp.stack([px, py, pz, core]).astype(jnp.int32)
    segment = segment_rows(lengths, assignment, ((px * 4 + py) * 4 + pz) * 2 + core, ROWS)
    seg_col, seg_row = segment.reshape(ROWS, 1), segment.reshape(1, ROWS)
    turned = hidden_in.T
    q, k, v, lse, ctx, n1, low, low_t, inv, vec, bi = attend(hidden_in, seg_col, seg_row, gathered)
    turned_2, ctx_2, low_2 = swap(turned), swap(ctx), swap(low_t)
    act, slope, layer_out, dsec, dbr, two = forward(
        low, n1, seg_col, out_cotangent, vec, bi, gathered
    )
    act, dbr, turned_2, ctx_2, low_2 = together(act, dbr, turned_2, ctx_2, low_2)
    act_2, dbr_2 = swap(act), swap(dbr)
    dpre, dbi, acc = backward_one(dbr, slope, dsec, gathered)
    act_2, dbr_2, acc = together(act_2, dbr_2, acc)
    back = back_grad(place, act, act_2, dbr, dbr_2)
    back, acc = together(back, acc)
    near = to_near(back)
    dpre, dbi, dfirst, dattn, dctx, one = backward_two(
        dbr, slope, acc, n1, inv, vec, dpre, dbi, gathered
    )
    near, dpre, dattn, dctx = together(near, dpre, dattn, dctx)
    far = to_far(back)
    dpre_2, dattn_2 = swap(dpre), swap(dattn)
    left, sums_l, acc = attend_back(0, q, k, v, dctx, lse, seg_col, seg_row, dfirst, gathered)
    far, dpre_2, dattn_2, left, acc = together(far, dpre_2, dattn_2, left, acc)
    back = arrived(back, near, far)
    left_2 = swap(left)
    middle = middle_grad(
        place, low_t, low_2, dpre, dpre_2, ctx, ctx_2, dattn, dattn_2, two, dbi, one
    )
    left_2, middle, acc = together(left_2, middle, acc)
    near = to_near(middle)
    right, sums_r, input_grad = attend_back(
        1, q, k, v, dctx, lse, seg_col, seg_row, acc, gathered
    )
    near, right, back = together(near, right, back)
    far = to_far(middle)
    right_2 = swap(right)
    back = ring_sum(place, back)
    back, right_2 = together(back, right_2)
    late = qkv_grad(place, turned, turned_2, left, left_2, right, right_2, sums_l, sums_r)
    far, late = together(far, late)
    middle = arrived(middle, near, far)
    late = arrived(late, to_near(late), to_far(late))
    parts = second_rings(ring_sum(place, [*back, *middle, *late]))
    weights, s = finish(place, core, parts)
    return (
        layer_out,
        input_grad,
        weights[0],
        s["bq"],
        s["bv"],
        weights[1],
        s["bo"],
        s["g1"],
        s["s1"],
        weights[2],
        s["bi"],
        weights[3],
        s["bb"],
        s["g2"],
        s["s2"],
    )


def solution(mesh):
    axes = ("x", "y", "z", "c")
    grid = Mesh(mesh.devices.reshape(4, 4, 4, 2), axes)
    two, one, every = P(axes, None), P(axes), P()
    in_specs = (two, two, every, every, two, one, one, two, one, one, one, two, one, two)
    in_specs = in_specs + (one, one, one)
    out_specs = (two, two, two, one, one, two, one, one, one, two, one, two, one, one, one)
    return jax.shard_map(body, mesh=grid, in_specs=in_specs, out_specs=out_specs, check_vma=False)
```

```python
import functools

import jax
import jax.numpy as jnp
from jax import lax
from jax.experimental import pallas as pl
from jax.experimental.pallas import tpu as pltpu
from jax.sharding import Mesh, PartitionSpec as P

ROWS = 512
D = 768
FF = 3072
LANES = 128
EPSILON = 1e-05
SCALE = 0.125
MASK_FILL = -1000000000.0
bf16, f32 = jnp.bfloat16, jnp.float32
NAMES = ("bq", "bv", "bo", "g1", "s1", "bi", "bb", "g2", "s2")
CUTS = dict(zip(NAMES, (6, 6, 6, 6, 6, 24, 6, 6, 6)))
AT = dict(zip(NAMES, (0, 6, 12, 18, 24, 30, 54, 60, 66)))
ROW_OF = dict(bq=0, bv=1, bo=2, g1=3, s1=4, bb=5, g2=6, s2=7)
LAST = (((1,), (1,)), ((), ()))
FIRST = (((0,), (0,)), ((), ()))


def shape(dims, kind=f32):
    return jax.ShapeDtypeStruct(dims, kind)


def whole(dims):
    return pl.BlockSpec(dims, lambda *_: (0,) * len(dims), pipeline_mode=pl.Buffered(1))


def kept(dims):
    return pl.BlockSpec(dims, lambda *_: (0,) * len(dims))


def run(kernel, grid, ins, outs, shapes, scratch=(), scalars=0, flops=0, size=0, alias=None):
    return pl.pallas_call(
        kernel,
        grid_spec=pltpu.PrefetchScalarGridSpec(
            num_scalar_prefetch=scalars,
            grid=grid,
            in_specs=ins,
            out_specs=outs,
            scratch_shapes=scratch,
        ),
        out_shape=shapes,
        input_output_aliases=alias or {},
        compiler_params=pltpu.CompilerParams(vmem_limit_bytes=63 * 1024 * 1024),
        cost_estimate=pl.CostEstimate(flops=flops, bytes_accessed=size, transcendentals=0),
    )


def mul(a, b, dims=(((1,), (0,)), ((), ()))):
    return lax.dot_general(a, b, dims, preferred_element_type=f32)


def shifted(n, step):
    return [(i, (i + step) % n) for i in range(n)]


def pack_kernel(place, qkv, out, inw, back, row, keep_o, send_o):
    halves = []
    for half in range(2):
        blocks = [(qkv, 6 * t + 3 * half + j) for t in range(3) for j in range(3)]
        blocks += [(out, 3 * half + j) for j in range(3)]
        blocks += [(inw, 12 * half + j) for j in range(12)]
        blocks += [(back, 3 * half + j) for j in range(3)]
        parts = [ref[:, LANES * j : LANES * (j + 1)].astype(f32) for ref, j in blocks]
        parts += [row[...].astype(f32), jnp.zeros((7, LANES), f32)]
        halves.append(jnp.concatenate(parts, axis=0).astype(bf16))
    for core in range(2):

        @pl.when(place[3] == core)
        def _():
            keep_o[...], send_o[...] = halves[core], halves[1 - core]


def pack(place, qkv, out, inw, back, row):
    arrays = (qkv, out, inw, back, row)
    return run(
        pack_kernel,
        (1,),
        [kept(a.shape) for a in arrays],
        [kept((224, LANES))] * 2,
        [shape((224, LANES), bf16)] * 2,
        scalars=1,
    )(place, *arrays)


def tile_kernel(place, *refs):
    ins, (one_o, two_o, rest_o, near) = refs[:4], refs[4:]
    core = place[3]
    for ref, k in zip(ins, (0, 1, 3, 2)):
        z = (place[2] + 4 - k) % 4
        near[z, core] = ref[:224, :].astype(f32)
        near[z, 1 - core] = ref[224:, :].astype(f32)

    def block(first, height):
        parts = [near[z, c, first : first + height, :] for z in range(4) for c in range(2)]
        return jnp.concatenate(parts, axis=0)

    head = [block(6 * i, 6) for i in range(12)] + [block(216, 1), jnp.zeros((8, LANES), f32)]
    head = jnp.concatenate(head, axis=0).astype(bf16)
    one_o[...], two_o[...] = head[:304], head[304:]
    rest = [block(6 * i, 6) for i in range(12, 24)] + [block(144 + 24 * j, 24) for j in range(3)]
    rest_o[...] = jnp.concatenate(rest, axis=0).astype(bf16)


def tile(place, parts):
    return run(
        tile_kernel,
        (1,),
        [kept((448, LANES))] * 4,
        [kept((304, LANES)), kept((288, LANES)), kept((1152, LANES))],
        [shape((304, LANES), bf16), shape((288, LANES), bf16), shape((1152, LANES), bf16)],
        [pltpu.VMEM((4, 2, 224, LANES), f32)],
        scalars=1,
    )(place, *parts)


def line_kernel(place, *refs):
    ins, outs = refs[:8], refs[8:]
    for out, first, at in ((outs[0], 0, place[0]), (outs[1], 4, place[1])):
        for i, k in enumerate((0, 1, 3, 2)):
            out[(at + 4 - k) % 4] = ins[first + i][...]


def line(place, parts):
    outs = [(4, *parts[0].shape), (4, *parts[4].shape)]
    return run(
        line_kernel,
        (1,),
        [kept(p.shape) for p in parts],
        [kept(o) for o in outs],
        [shape(o, bf16) for o in outs],
        scalars=1,
    )(place, *parts)


def plane_kernel(place, *refs):
    ins, out = refs[:8], refs[8]
    rows = ins[0].shape[1]
    for i, k in enumerate((0, 1, 3, 2)):
        x, y = (place[0] + 4 - k) % 4, (place[1] + 4 - k) % 4
        for j in range(4):
            out[4 * j + y, :rows, :] = ins[i][j]
            out[4 * x + j, rows:, :] = ins[4 + i][j]


def plane(place, parts):
    rows = parts[0].shape[1] + parts[4].shape[1]
    return run(
        plane_kernel,
        (1,),
        [kept(p.shape) for p in parts],
        kept((16, rows, LANES)),
        shape((16, rows, LANES), bf16),
        scalars=1,
    )(place, *parts)


def spread_along(value, axis):
    return [value] + [lax.ppermute(value, axis, shifted(4, k)) for k in (1, 3, 2)]


def gather_all(place, qkv, out, inw, back, small):
    row = sum(jnp.pad(v, (AT[n], LANES - AT[n] - CUTS[n])) for n, v in zip(NAMES, small))[None]
    keep, send = pack(place, qkv, out, inw, back, row)
    pair = jnp.concatenate([keep, swap(send)], axis=0)
    one, two, rest = tile(place, spread_along(pair, "z"))
    rest = lax.all_gather(rest, ("x", "y", "c"), tiled=False).reshape(16, 2, 1152, LANES)
    one, two = line(place, spread_along(one, "x") + spread_along(two, "y"))
    own = plane(place, spread_along(one, "y") + spread_along(two, "x"))
    return own, swap(own), rest


def chosen(here, own, other):
    rows = own.shape[0] * 48
    blocks = own.shape[1] // 48

    def of(ref):
        parts = [ref[:, 48 * j : 48 * (j + 1), :].reshape(rows, LANES) for j in range(blocks)]
        return parts[0] if blocks == 1 else jnp.concatenate(parts, axis=1)

    return lax.cond(here, lambda: of(own), lambda: of(other))


def held_columns(ref, block):
    rows = pl.ds(pl.multiple_of(48 * block, 16), 48)
    return ref[:, rows, :].reshape(D, LANES)


def out_columns(core, own, other):
    left, right = chosen(core == 0, own, other), chosen(core == 1, own, other)
    return jnp.concatenate([left, right], axis=1)


def columns(ref, count, height=48, halves=(0,)):
    rows = ref.shape[0] * height
    parts = [
        ref[:, half, height * j : height * (j + 1), :].reshape(rows, LANES)
        for half in halves
        for j in range(count)
    ]
    return parts[0] if len(parts) == 1 else jnp.concatenate(parts, axis=1)


OUT = pl.BlockSpec((16, 144, LANES), lambda *_: (0, 3, 0), pipeline_mode=pl.Buffered(1))
IN = pl.BlockSpec((16, 1, 144, LANES), lambda b: (0, b // 4, b % 4, 0))
BACK = pl.BlockSpec((2, 2, 576, LANES), lambda b: (b, 0, 1, 0))
ANYWHERE = pl.BlockSpec(memory_space=pl.ANY)
PAIR = pl.BlockSpec((ROWS, LANES), lambda p, *_: (0, p))
WIDE = pl.BlockSpec((ROWS, 384), lambda b: (0, b))


def place_of(cut, shape_, dim):
    at = lax.broadcasted_iota(jnp.int32, shape_, dim)
    owner = (at * (10923 if cut == 6 else 2731)) >> 16
    return owner, at - owner * cut


def spread(rows, name):
    cut = CUTS[name]
    width = cut * 128
    _, place = place_of(cut, (LANES, width), 1)
    pick = lax.broadcasted_iota(jnp.int32, (LANES, width), 0) == place + AT[name]
    every = mul(rows, jnp.where(pick, 1.0, 0.0).astype(bf16))
    owner, _ = place_of(cut, (128, width), 1)
    here = lax.broadcasted_iota(jnp.int32, (128, width), 0) == owner
    return jnp.sum(jnp.where(here, every, 0.0), axis=0, keepdims=True)


def gathered_rows(vectors):
    total = jnp.zeros((128, LANES), f32)
    for name, vector in vectors:
        cut = CUTS[name]
        width = cut * 128
        owner, _ = place_of(cut, (128, width), 1)
        here = lax.broadcasted_iota(jnp.int32, (128, width), 0) == owner
        _, place = place_of(cut, (width, LANES), 0)
        pick = lax.broadcasted_iota(jnp.int32, (width, LANES), 1) == place + AT[name]
        own = jnp.where(here, vector, 0.0).astype(bf16)
        total = total + mul(own, jnp.where(pick, 1.0, 0.0).astype(bf16))
    total = total.reshape(16, 8, LANES)
    return jnp.concatenate([total, jnp.zeros((16, 8, LANES), f32)], axis=1).astype(bf16)


def normalise(total):
    centred = total - jnp.mean(total, axis=-1, keepdims=True)
    inverse = lax.rsqrt(jnp.mean(centred * centred, axis=-1, keepdims=True) + EPSILON)
    return centred * inverse, inverse


def norm_back(grad, normed, inverse, gain):
    scaled = grad * gain
    mean = jnp.mean(scaled, axis=-1, keepdims=True)
    slope = jnp.mean(scaled * normed, axis=-1, keepdims=True)
    return inverse * (scaled - mean - normed * slope)


def column_sum(value):
    return jnp.sum(value, axis=0, keepdims=True)


def head_mask(head):
    lane = lax.broadcasted_iota(jnp.int32, (ROWS, LANES), 1)
    return (lane < 64) if head == 0 else (lane >= 64)


def masked(value, head, factor=1.0):
    return jnp.where(head_mask(head), value.astype(f32) * factor, 0.0).astype(bf16)


def attend_kernel(
    place, x, sc, sr, own, other, q_o, k_o, v_o, lse_o, ctx_o, n1_o, low_o, turn_o, inv_o, vec_o,
    bin_o, bias, ctx_s, held, arrived_s,
):
    p = pl.program_id(0)

    @pl.when(p == 0)
    def _():
        core = place[3]
        copies = [
            pltpu.make_async_copy(own, held.at[core], arrived_s.at[0]),
            pltpu.make_async_copy(other, held.at[1 - core], arrived_s.at[1]),
        ]
        for copy in copies:
            copy.start()
        bias[...] = jnp.where(sc[...] == sr[...], 0.0, MASK_FILL)
        for copy in copies:
            copy.wait()
        rows = held[0, :, 576:592, :].astype(f32)[:, :8, :].reshape(128, LANES).astype(bf16)
        for name, row in ROW_OF.items():
            vec_o[row : row + 1, :] = spread(rows, name)
        bin_o[0:1, :] = spread(rows, "bi")

    weights = [held_columns(held.at[p // 3], 3 * t + p % 3) for t in range(3)]
    mixed = mul(x[...], jnp.concatenate(weights, axis=1))
    lanes = pl.ds(pl.multiple_of(p * LANES, LANES), LANES)
    q = (mixed[:, :LANES] + vec_o[0:1, lanes]).astype(bf16)
    k = mixed[:, LANES : 2 * LANES].astype(bf16)
    value = (mixed[:, 2 * LANES :] + vec_o[1:2, lanes]).astype(bf16)
    q_o[...], k_o[...], v_o[...] = q, k, value
    turned = value.astype(f32).T.astype(bf16)
    parts = []
    for head in range(2):
        scores = mul(k, masked(q, head, SCALE), LAST) + bias[...]
        top = jnp.max(scores, axis=0, keepdims=True)
        raised = jnp.exp(scores - top)
        total = jnp.sum(raised, axis=0, keepdims=True)
        lse_o[0, head : head + 1, :] = top + jnp.log(total)
        probs = (raised * (1.0 / total)).astype(bf16)
        parts.append(mul(turned[64 * head : 64 * (head + 1)], probs))
    context = jnp.concatenate(parts, axis=0)
    ctx_o[...] = context.astype(bf16)
    ctx_s[:, lanes] = context.T.astype(bf16)

    @pl.when(p == 5)
    def _():
        weights = [held_columns(held.at[h], 9 + j) for h in range(2) for j in range(3)]
        attn = mul(ctx_s[...], jnp.concatenate(weights, axis=1)) + vec_o[2:3, :]
        normed, inverse = normalise(x[...].astype(f32) + attn)
        n1_o[...], inv_o[...] = normed, inverse
        first = normed * vec_o[3:4, :] + vec_o[4:5, :]
        low_o[...], turn_o[...] = first.astype(bf16), first.T.astype(bf16)


def attend(place, x, seg_col, seg_row, own, other):
    wide, tall, pair = shape((ROWS, D), bf16), shape((D, ROWS), bf16), PAIR
    return run(
        attend_kernel,
        (6,),
        [whole((ROWS, D)), whole((ROWS, 1)), whole((1, ROWS)), ANYWHERE, ANYWHERE],
        [pair, pair, pair, pl.BlockSpec((1, 8, ROWS), lambda p, *_: (p, 0, 0))]
        + [pl.BlockSpec((LANES, ROWS), lambda p, *_: (p, 0)), kept((ROWS, D)), kept((ROWS, D))]
        + [kept((D, ROWS)), kept((ROWS, 1)), kept((8, D)), kept((8, FF))],
        [wide, wide, wide, shape((6, 8, ROWS)), tall, shape((ROWS, D)), wide, tall]
        + [shape((ROWS, 1)), shape((8, D)), shape((8, FF))],
        [pltpu.VMEM((ROWS, ROWS), f32), pltpu.VMEM((ROWS, D), bf16)]
        + [pltpu.VMEM((2, 16, 592, LANES), bf16), pltpu.SemaphoreType.DMA((2,))],
        scalars=1,
        flops=6_000_000_000,
        size=12_000_000,
    )(place, x, seg_col, seg_row, own, other)


def forward_kernel(
    low, n1, sc, cot, vec, bi, wi, wb, act_o, slope_o, out_o, dsec_o, dbr_o, sums_o, acc
):
    b = pl.program_id(0)
    pre = mul(low[...], columns(wi, 3)) + bi[0:1, :]
    share = 0.5 * lax.erf(pre * 0.7071067811865476) + 0.5
    act = pre * share
    act_o[...] = act.T.astype(bf16)
    act = act.astype(bf16)
    slope_o[...] = (share + pre * (jnp.exp(pre * pre * -0.5) * 0.3989422804014327)).astype(bf16)
    term = mul(act, columns(wb, 3, 192, (0, 1)))

    @pl.when(b == 0)
    def _():
        acc[...] = term

    @pl.when(b > 0)
    def _():
        acc[...] += term

    @pl.when(b == 7)
    def _():
        first = n1[...] * vec[3:4, :] + vec[4:5, :]
        normed, inverse = normalise(first + (acc[...] + vec[5:6, :]))
        valid = jnp.where(sc[...] > 0, 1.0, 0.0)
        out_o[...] = ((normed * vec[6:7, :] + vec[7:8, :]) * valid).astype(bf16)
        grad = cot[...].astype(f32) * valid
        sums_o[0:1, :] = column_sum(grad * normed)
        sums_o[1:2, :] = column_sum(grad)
        second = norm_back(grad, normed, inverse, vec[6:7, :])
        dsec_o[...] = second
        rounded = second.astype(bf16)
        dbr_o[...] = rounded
        sums_o[2:3, :] = column_sum(rounded.astype(f32))


def forward(low, n1, seg_col, cot, vec, bi, gathered):
    deep, wide = shape((ROWS, FF), bf16), shape((ROWS, D), bf16)
    flat = whole((ROWS, D))
    return run(
        forward_kernel,
        (8,),
        [flat, flat, whole((ROWS, 1)), flat, whole((8, D))]
        + [pl.BlockSpec((8, 384), lambda b: (0, b)), IN, BACK],
        [pl.BlockSpec((384, ROWS), lambda b: (b, 0)), WIDE]
        + [kept((ROWS, D)), kept((ROWS, D)), kept((ROWS, D)), kept((8, D))],
        [shape((FF, ROWS), bf16), deep, wide, shape((ROWS, D)), wide, shape((8, D))],
        [pltpu.VMEM((ROWS, D), f32)],
        flops=10_000_000_000,
        size=20_000_000,
    )(low, n1, seg_col, cot, vec, bi, gathered, gathered)


def backward_one_kernel(dbr, slope, dsec, wi, wb, dpre_o, bi_o, acc):
    b = pl.program_id(0)
    dact = mul(dbr[...], columns(wb, 3, 192, (0, 1)), LAST)
    dpre = (dact * slope[...].astype(f32)).astype(bf16)
    dpre_o[...] = dpre
    bi_o[0:1, :] = column_sum(dpre.astype(f32))
    term = mul(dpre, columns(wi, 3), LAST)

    @pl.when(b == 0)
    def _():
        acc[...] = dsec[...] + term

    @pl.when(b > 0)
    def _():
        acc[...] += term


def backward_two_kernel(
    place, dbr, slope, dsec, wi, wb, wo, wo_2, n1, inv, vec, dpre_in, bi_in, dpre_o, bi_o, dfirst_o,
    dattn_o, dctx_o, sums_o, acc,
):
    backward_one_kernel(dbr, slope, dsec, wi, wb, dpre_o, bi_o, acc)

    @pl.when(pl.program_id(0) == 3)
    def _():
        grad, normed = acc[...], n1[...]
        sums_o[0:1, :] = column_sum(grad * normed)
        sums_o[1:2, :] = column_sum(grad)
        first = norm_back(grad, normed, inv[...], vec[3:4, :])
        dfirst_o[...] = first
        rounded = first.astype(bf16)
        dattn_o[...] = rounded
        sums_o[2:3, :] = column_sum(rounded.astype(f32))
        dctx_o[...] = mul(rounded, out_columns(place[3], wo, wo_2), LAST).astype(bf16)


def backward_specs(half):
    ins = [
        whole((ROWS, D)),
        pl.BlockSpec((ROWS, 384), lambda b, *_: (0, 4 * half + b)),
        whole((ROWS, D)),
        pl.BlockSpec((16, 1, 144, LANES), lambda b, *_: (0, half, b, 0)),
        pl.BlockSpec((2, 2, 576, LANES), lambda b, *_: (4 * half + b, 0, 1, 0)),
    ]
    outs = [
        pl.BlockSpec((ROWS, 384), lambda b, *_: (0, 4 * half + b)),
        pl.BlockSpec((8, 384), lambda b, *_: (0, 4 * half + b)),
    ]
    return ins, outs, [shape((ROWS, FF), bf16), shape((8, FF))]


def backward_one(dbr, slope, dsec, gathered):
    ins, outs, shapes = backward_specs(0)
    return run(
        backward_one_kernel,
        (4,),
        ins,
        outs + [kept((ROWS, D))],
        shapes + [shape((ROWS, D))],
        flops=5_000_000_000,
        size=10_000_000,
    )(dbr, slope, dsec, gathered, gathered)


def backward_two(place, dbr, slope, acc, n1, inv, vec, dpre, bi, gathered, own, other):
    wide, flat = shape((ROWS, D), bf16), whole((ROWS, D))
    ins, outs, shapes = backward_specs(1)
    return run(
        backward_two_kernel,
        (4,),
        ins + [OUT, OUT, flat, whole((ROWS, 1)), whole((8, D)), ANYWHERE, ANYWHERE],
        outs + [kept((ROWS, D)), kept((ROWS, D)), kept((ROWS, D)), kept((8, D))],
        shapes + [shape((ROWS, D)), wide, wide, shape((8, D))],
        [pltpu.VMEM((ROWS, D), f32)],
        flops=6_000_000_000,
        size=10_000_000,
        alias={11: 0, 12: 1},
        scalars=1,
    )(place, dbr, slope, acc, gathered, gathered, own, other, n1, inv, vec, dpre, bi)


def attend_back_kernel(
    half, place, q, k, v, dctx, lse, sc, sr, dfirst, own, other, mixed_o, sums_o, dx_o, bias, acc,
    held, arrived_s,
):
    p = pl.program_id(0)

    @pl.when(p == 0)
    def _():
        bias[...] = jnp.where(sc[...] == sr[...], 0.0, MASK_FILL)
        acc[...] = dfirst[...]
        for here, source in ((half, own), (1 - half, other)):

            @pl.when(place[3] == here)
            def _():
                copy = pltpu.make_async_copy(source.at[:, :432, :], held, arrived_s.at[0])
                copy.start()
                copy.wait()

    key, value = k[...], v[...]
    turned = key.astype(f32).T.astype(bf16)
    dk = jnp.zeros((ROWS, LANES), f32)
    dv = jnp.zeros((ROWS, LANES), f32)
    parts = []
    for head in range(2):
        query = masked(q[...], head, SCALE)
        grad = masked(dctx[...], head)
        probs = jnp.exp(mul(key, query, LAST) + bias[...] - lse[0, head : head + 1, :])
        dprobs = mul(value, grad, LAST)
        dv = dv + mul(probs.astype(bf16), grad)
        dscores = (probs * (dprobs - column_sum(probs * dprobs))).astype(bf16)
        dk = dk + mul(dscores, query)
        parts.append(mul(turned[64 * head : 64 * (head + 1)], dscores))
    dq = (jnp.concatenate(parts, axis=0).T * SCALE).astype(bf16)
    dk, dv = dk.astype(bf16), dv.astype(bf16)
    mixed_o[0], mixed_o[1], mixed_o[2] = dq, dk, dv
    sums_o[0:1, :] = column_sum(dq.astype(f32))
    sums_o[1:2, :] = column_sum(dv.astype(f32))
    weight = jnp.concatenate([held_columns(held, 3 * t + p) for t in range(3)], axis=1)
    acc[...] += mul(jnp.concatenate([dq, dk, dv], axis=1), weight, LAST)

    @pl.when(p == 2)
    def _():
        dx_o[...] = acc[...].astype(dx_o.dtype)


def attend_back(half, place, q, k, v, dctx, lse, seg_col, seg_row, dfirst, own, other):
    pair = pl.BlockSpec((ROWS, LANES), lambda p, *_: (0, 3 * half + p))
    return run(
        functools.partial(attend_back_kernel, half),
        (3,),
        [pair, pair, pair, pair, pl.BlockSpec((1, 8, ROWS), lambda p, *_: (3 * half + p, 0, 0))]
        + [whole((ROWS, 1)), whole((1, ROWS)), whole((ROWS, D)), ANYWHERE, ANYWHERE],
        [pl.BlockSpec((3, ROWS, LANES), lambda p, *_: (0, 0, p))]
        + [pl.BlockSpec((8, LANES), lambda p, *_: (0, p)), kept((ROWS, D))],
        [shape((3, ROWS, 384), bf16), shape((8, 384)), shape((ROWS, D), (f32, bf16)[half])],
        [pltpu.VMEM((ROWS, ROWS), f32), pltpu.VMEM((ROWS, D), f32)]
        + [pltpu.VMEM((16, 432, LANES), bf16), pltpu.SemaphoreType.DMA((1,))],
        scalars=1,
        flops=6_000_000_000,
        size=8_000_000,
    )(place, q, k, v, dctx, lse, seg_col, seg_row, dfirst, own, other)


def put(total, at, grad):
    rows = grad.astype(bf16).reshape(16, 48, -1)
    for j in range(rows.shape[2] // LANES):
        total[:, pl.ds(at + 48 * j, 48), :] = rows[:, :, LANES * j : LANES * (j + 1)]


def back_grad_kernel(place, act, act_2, dbr, dbr_2, total):
    grad = (mul(act[...], dbr[...]) + mul(act_2[...], dbr_2[...])).astype(bf16)
    for at in range(2):
        for j in range(3):
            part = grad[192 * at : 192 * (at + 1), LANES * j : LANES * (j + 1)]
            total[at, 192 * j : 192 * (j + 1), :] = part

def back_grad(place, act, act_2, dbr, dbr_2):
    tall = pl.BlockSpec((384, ROWS), lambda b, p: (b, 0))
    half = pl.BlockSpec((ROWS, 384), lambda b, p: (0, p[3]))
    return run(
        back_grad_kernel,
        (8,),
        [tall, tall, half, half],
        pl.BlockSpec((2, 576, LANES), lambda b, p: (b, 0, 0)),
        shape((16, 576, LANES), bf16),
        scalars=1,
        flops=2_400_000_000,
        size=10_000_000,
    )(place, act, act_2, dbr, dbr_2)


def middle_grad_kernel(
    place, low, low_2, dpre, dpre_2, ctx, ctx_2, dattn, dattn_2, two, bi, one, total
):
    b = pl.program_id(0)

    @pl.when(b < 4)
    def _():
        grad = mul(low[...], dpre[...]) + mul(low_2[...], dpre_2[...])
        put(total, pl.multiple_of(144 * b, 16), grad)

    @pl.when(b == 4)
    def _():
        put(total, 576, mul(ctx[...], dattn[...]) + mul(ctx_2[...], dattn_2[...]))
        names = (("g2", two, 0), ("s2", two, 1), ("bb", two, 2), ("bi", bi, 0))
        names = names + (("g1", one, 0), ("s1", one, 1), ("bo", one, 2))
        total[:, 720:736, :] = gathered_rows([(n, ref[i : i + 1, :]) for n, ref, i in names])


def middle_grad(place, low, low_2, dpre, dpre_2, ctx, ctx_2, dattn, dattn_2, two, bi, one):
    tall = whole((D, ROWS))
    quarter = pl.BlockSpec((ROWS, 384), lambda b, p: (0, 4 * p[3] + jnp.minimum(b, 3)))
    half = pl.BlockSpec((ROWS, 384), lambda b, p: (0, p[3]))
    return run(
        middle_grad_kernel,
        (5,),
        [tall, tall, quarter, quarter, tall, tall, half, half]
        + [whole((8, D)), whole((8, FF)), whole((8, D))],
        kept((16, 736, LANES)),
        shape((16, 736, LANES), bf16),
        scalars=1,
        flops=3_200_000_000,
        size=12_000_000,
    )(place, low, low_2, dpre, dpre_2, ctx, ctx_2, dattn, dattn_2, two, bi, one)


def qkv_grad_kernel(place, x, x_2, left, left_2, right, right_2, sums_l, sums_r, total):
    for core, own, other in ((0, left, left_2), (1, right, right_2)):

        @pl.when(place[3] == core)
        def _():
            for t in range(3):
                put(total, 144 * t, mul(x[...], own[t]) + mul(x_2[...], other[t]))

    sums = [jnp.concatenate([sums_l[i : i + 1, :], sums_r[i : i + 1, :]], axis=1) for i in (0, 1)]
    total[:, 432:448, :] = gathered_rows([("bq", sums[0]), ("bv", sums[1])])


def qkv_grad(place, x, x_2, left, left_2, right, right_2, sums_l, sums_r):
    half = kept((3, ROWS, 384))
    return run(
        qkv_grad_kernel,
        (1,),
        [kept((D, ROWS)), kept((D, ROWS)), half, half, half, half, kept((8, 384)), kept((8, 384))],
        kept((16, 448, LANES)),
        shape((16, 448, LANES), bf16),
        scalars=1,
        flops=1_800_000_000,
        size=7_000_000,
    )(place, x, x_2, left, left_2, right, right_2, sums_l, sums_r)


def last_kernel(place, *refs):
    early, late, outs = refs[0], refs[1], refs[2:]
    back, middle = early[:576, :].astype(f32), early[576:, :].astype(f32)
    qkv = late[0].astype(f32)
    for i in range(1, 16):
        qkv = qkv + late[i].astype(f32)
    wide = [qkv[48 * j : 48 * (j + 1)] for j in range(9)]
    wide = wide + [middle[576 + 48 * j : 576 + 48 * (j + 1)] for j in range(3)]
    wide = wide + [middle[48 * j : 48 * (j + 1)] for j in range(12)]
    rows = middle[720:728] + qkv[432:440]
    none = jnp.zeros((4, LANES), f32)
    for z in range(4):
        parts = []
        for block in wide:
            parts = parts + [block[12 * z : 12 * (z + 1)], none]
        for j in range(3):
            parts.append(back[192 * j + 48 * z : 192 * j + 48 * (z + 1)])
        parts = parts + [rows[2 * z : 2 * (z + 1)], jnp.zeros((14, LANES), f32)]
        total = jnp.concatenate(parts, axis=0).astype(bf16)
        for k in range(4):

            @pl.when((place[2] + k) % 4 == z)
            def _():
                outs[k][...] = total


def last_sum(place, parts):
    return run(
        last_kernel,
        (1,),
        [kept(p.shape) for p in parts],
        [kept((544, LANES))] * 4,
        [shape((544, LANES), bf16)] * 4,
        scalars=1,
        size=4_000_000,
    )(place, *parts)


def around(parts, axis):
    return [parts[0]] + [lax.ppermute(parts[k], axis, shifted(4, k)) for k in (1, 3, 2)]


def scattered(value, axis):
    return lax.psum_scatter(value, axis, tiled=True)


def swap(value):
    return lax.ppermute(value, "c", shifted(2, 1))


def together(*values):
    flat, tree = jax.tree.flatten(values)
    return jax.tree.unflatten(tree, lax.optimization_barrier(tuple(flat)))


def finish(place, core, parts):
    parts = around(last_sum(place, parts), "z")
    total = sum(p.astype(f32) for p in parts)
    wide = total[:384].reshape(24, 16, LANES)[:, :12].reshape(24, 2, 6, LANES)
    tall = total[384:528].reshape(3, 2, 24, LANES)

    def for_core(which):
        a = lax.dynamic_index_in_dim(wide, which, 1, keepdims=False).reshape(144, LANES)
        b = lax.dynamic_index_in_dim(tall, which, 1, keepdims=False).reshape(72, LANES)
        row = lax.dynamic_index_in_dim(total[528:530], which, 0)
        return jnp.concatenate([a, b, row], axis=0)

    own = for_core(core)
    other = lax.ppermute(for_core(1 - core).astype(bf16), "c", shifted(2, 1)).astype(f32)
    rows = own[216] + other[216]
    left, right = jnp.where(core == 0, own, other), jnp.where(core == 0, other, own)

    def joined(first, count, height, groups=1):
        parts = [
            jnp.moveaxis(a[first : first + count * height].reshape(count, height, LANES), 0, 1)
            for a in (left, right)
        ]
        parts = [p.reshape(height, groups, -1) for p in parts]
        return jnp.concatenate(parts, axis=2).reshape(height, -1)

    weights = joined(0, 9, 6, 3), joined(54, 3, 6), joined(72, 12, 6), joined(144, 3, 24)
    return weights, {n: rows[AT[n] : AT[n] + CUTS[n]] for n in NAMES}


def segment_rows(lengths, assignment, device, rows):
    count = lengths.shape[0]
    order = jnp.arange(count, dtype=jnp.int32)
    same = assignment[:, None] == assignment[None, :]
    before = order[None, :] < order[:, None]
    offset = jnp.sum(jnp.where(same & before, lengths[None, :], 0), axis=1)
    places = jnp.arange(rows, dtype=jnp.int32)[:, None]
    inside = (
        (assignment[None, :] == device)
        & (places >= offset[None, :])
        & (places < (offset + lengths)[None, :])
    )
    return jnp.sum(jnp.where(inside, order[None, :] + 1, 0), axis=1)


def body(
    hidden_in,
    out_cotangent,
    lengths,
    assignment,
    qkv_weight,
    query_bias,
    value_bias,
    out_weight,
    out_bias,
    first_gain,
    first_shift,
    in_weight,
    in_bias,
    back_weight,
    back_bias,
    second_gain,
    second_shift,
):
    small = [
        query_bias,
        value_bias,
        out_bias,
        first_gain,
        first_shift,
        in_bias,
        back_bias,
        second_gain,
        second_shift,
    ]
    px, py, pz, core = (lax.axis_index(a) for a in ("x", "y", "z", "c"))
    place = jnp.stack([px, py, pz, core]).astype(jnp.int32)
    own, other, gathered = gather_all(
        place, qkv_weight, out_weight, in_weight, back_weight, small
    )
    segment = segment_rows(lengths, assignment, ((px * 4 + py) * 4 + pz) * 2 + core, ROWS)
    seg_col, seg_row = segment.reshape(ROWS, 1), segment.reshape(1, ROWS)
    turned = hidden_in.T
    q, k, v, lse, ctx, n1, low, low_t, inv, vec, bi = attend(
        place, hidden_in, seg_col, seg_row, own, other
    )
    turned_2, ctx_2, low_2 = swap(turned), swap(ctx), swap(low_t)
    act, slope, layer_out, dsec, dbr, two = forward(
        low, n1, seg_col, out_cotangent, vec, bi, gathered
    )
    act, dbr, turned_2, ctx_2, low_2 = together(act, dbr, turned_2, ctx_2, low_2)
    act_2, dbr_2 = swap(act), swap(dbr)
    dpre, dbi, acc = backward_one(dbr, slope, dsec, gathered)
    act_2, dbr_2, acc = together(act_2, dbr_2, acc)
    back = back_grad(place, act, act_2, dbr, dbr_2)
    back, acc = together(back, acc)
    back = scattered(back.reshape(-1, LANES), "x")
    dpre, dbi, dfirst, dattn, dctx, one = backward_two(
        place, dbr, slope, acc, n1, inv, vec, dpre, dbi, gathered, own, other
    )
    dpre_2, dattn_2 = swap(dpre), swap(dattn)
    middle = middle_grad(
        place, low_t, low_2, dpre, dpre_2, ctx, ctx_2, dattn, dattn_2, two, dbi, one
    )
    middle, dctx = together(middle, dctx)
    middle = scattered(middle.reshape(-1, LANES), "x")
    left, sums_l, acc = attend_back(
        0, place, q, k, v, dctx, lse, seg_col, seg_row, dfirst, own, other
    )
    left_2 = swap(left)
    right, sums_r, input_grad = attend_back(
        1, place, q, k, v, dctx, lse, seg_col, seg_row, acc, own, other
    )
    left_2, right = together(left_2, right)
    right_2 = swap(right)
    late = qkv_grad(place, turned, turned_2, left, left_2, right, right_2, sums_l, sums_r)
    back, middle, late = together(back, middle, late)
    early = [back.reshape(4, 576, LANES), middle.reshape(4, 736, LANES)]
    early, late = together(jnp.concatenate(early, axis=1).reshape(-1, LANES), late)
    parts = [scattered(early, "y"), lax.all_to_all(late, ("x", "y"), 0, 0, tiled=True)]
    weights, s = finish(place, core, parts)
    return (
        layer_out,
        input_grad,
        weights[0],
        s["bq"],
        s["bv"],
        weights[1],
        s["bo"],
        s["g1"],
        s["s1"],
        weights[2],
        s["bi"],
        weights[3],
        s["bb"],
        s["g2"],
        s["s2"],
    )


def solution(mesh):
    axes = ("x", "y", "z", "c")
    grid = Mesh(mesh.devices.reshape(4, 4, 4, 2), axes)
    two, one, every = P(axes, None), P(axes), P()
    in_specs = (two, two, every, every, two, one, one, two, one, one, one, two, one, two)
    in_specs = in_specs + (one, one, one)
    out_specs = (two, two, two, one, one, two, one, one, one, two, one, two, one, one, one)
    return jax.shard_map(body, mesh=grid, in_specs=in_specs, out_specs=out_specs, check_vma=False)
```

```python
import functools

import jax
import jax.numpy as jnp
from jax import lax
from jax.experimental import pallas as pl
from jax.experimental.pallas import tpu as pltpu
from jax.sharding import Mesh, PartitionSpec as P

ROWS = 512
STEP = 768
D = 768
FF = 3072
LANES = 128
EPSILON = 1e-05
SCALE = 0.125
MASK_FILL = -1000000000.0
bf16, f32 = jnp.bfloat16, jnp.float32
NAMES = ("bq", "bv", "bo", "g1", "s1", "bi", "bb", "g2", "s2")
CUTS = dict(zip(NAMES, (6, 6, 6, 6, 6, 24, 6, 6, 6)))
AT = dict(zip(NAMES, (0, 6, 12, 18, 24, 30, 54, 60, 66)))
ROW_OF = dict(bq=0, bv=1, bo=2, g1=3, s1=4, bb=5, g2=6, s2=7)
LAST = (((1,), (1,)), ((), ()))
FIRST = (((0,), (0,)), ((), ()))


def shape(dims, kind=f32):
    return jax.ShapeDtypeStruct(dims, kind)


def whole(dims):
    return pl.BlockSpec(dims, lambda *_: (0,) * len(dims), pipeline_mode=pl.Buffered(1))


def kept(dims):
    return pl.BlockSpec(dims, lambda *_: (0,) * len(dims))


def run(kernel, grid, ins, outs, shapes, scratch=(), scalars=0, flops=0, size=0, alias=None):
    return pl.pallas_call(
        kernel,
        grid_spec=pltpu.PrefetchScalarGridSpec(
            num_scalar_prefetch=scalars,
            grid=grid,
            in_specs=ins,
            out_specs=outs,
            scratch_shapes=scratch,
        ),
        out_shape=shapes,
        input_output_aliases=alias or {},
        compiler_params=pltpu.CompilerParams(vmem_limit_bytes=64 * 1024 * 1024),
        cost_estimate=pl.CostEstimate(flops=flops, bytes_accessed=size, transcendentals=0),
    )


def mul(a, b, dims=(((1,), (0,)), ((), ()))):
    return lax.dot_general(a, b, dims, preferred_element_type=f32)


def shifted(n, step):
    return [(i, (i + step) % n) for i in range(n)]


def pack_kernel(place, qkv, out, inw, back, row, keep_o, send_o):
    halves = []
    for half in range(2):
        blocks = [(qkv, 6 * t + 3 * half + j) for t in range(3) for j in range(3)]
        blocks += [(out, 3 * half + j) for j in range(3)]
        blocks += [(inw, 12 * half + j) for j in range(12)]
        blocks += [(back, 3 * half + j) for j in range(3)]
        parts = [ref[:, LANES * j : LANES * (j + 1)].astype(f32) for ref, j in blocks]
        parts += [row[...].astype(f32), jnp.zeros((7, LANES), f32)]
        halves.append(jnp.concatenate(parts, axis=0).astype(bf16))
    for core in range(2):

        @pl.when(place[3] == core)
        def _():
            keep_o[...], send_o[...] = halves[core], halves[1 - core]


def pack(place, qkv, out, inw, back, row):
    arrays = (qkv, out, inw, back, row)
    return run(
        pack_kernel,
        (1,),
        [kept(a.shape) for a in arrays],
        [kept((224, LANES))] * 2,
        [shape((224, LANES), bf16)] * 2,
        scalars=1,
    )(place, *arrays)


def tile_kernel(place, *refs):
    ins, (one_o, two_o, rest_o, near) = refs[:4], refs[4:]
    core = place[3]
    for ref, k in zip(ins, (0, 1, 3, 2)):
        z = (place[2] + 4 - k) % 4
        near[z, core] = ref[:224, :].astype(f32)
        near[z, 1 - core] = ref[224:, :].astype(f32)

    def block(first, height):
        parts = [near[z, c, first : first + height, :] for z in range(4) for c in range(2)]
        return jnp.concatenate(parts, axis=0)

    head = [block(6 * i, 6) for i in range(9)] + [block(216, 1), jnp.zeros((8, LANES), f32)]
    head = jnp.concatenate(head, axis=0).astype(bf16)
    one_o[...], two_o[...] = head[:224], head[224:]
    rest = [block(6 * i, 6) for i in range(12, 24)] + [block(144 + 24 * j, 24) for j in range(3)]
    rest = rest + [block(6 * i, 6) for i in range(9, 12)]
    rest_o[...] = jnp.concatenate(rest, axis=0).astype(bf16)


def tile(place, parts):
    return run(
        tile_kernel,
        (1,),
        [kept((448, LANES))] * 4,
        [kept((224, LANES)), kept((224, LANES)), kept((1296, LANES))],
        [shape((224, LANES), bf16), shape((224, LANES), bf16), shape((1296, LANES), bf16)],
        [pltpu.VMEM((4, 2, 224, LANES), f32)],
        scalars=1,
    )(place, *parts)


def line_kernel(place, *refs):
    ins, outs = refs[:8], refs[8:]
    for out, first, at in ((outs[0], 0, place[0]), (outs[1], 4, place[1])):
        for i, k in enumerate((0, 1, 3, 2)):
            out[(at + 4 - k) % 4] = ins[first + i][...]


def line(place, parts):
    outs = [(4, *parts[0].shape), (4, *parts[4].shape)]
    return run(
        line_kernel,
        (1,),
        [kept(p.shape) for p in parts],
        [kept(o) for o in outs],
        [shape(o, bf16) for o in outs],
        scalars=1,
    )(place, *parts)


def plane_kernel(place, *refs):
    ins, out = refs[:8], refs[8]
    rows = ins[0].shape[1]
    for i, k in enumerate((0, 1, 3, 2)):
        x, y = (place[0] + 4 - k) % 4, (place[1] + 4 - k) % 4
        for j in range(4):
            out[4 * j + y, :rows, :] = ins[i][j]
            out[4 * x + j, rows:, :] = ins[4 + i][j]


def plane(place, parts):
    rows = parts[0].shape[1] + parts[4].shape[1]
    return run(
        plane_kernel,
        (1,),
        [kept(p.shape) for p in parts],
        kept((16, rows, LANES)),
        shape((16, rows, LANES), bf16),
        scalars=1,
    )(place, *parts)


def spread_along(value, axis):
    return [value] + [lax.ppermute(value, axis, shifted(4, k)) for k in (1, 3, 2)]


def gather_all(place, qkv, out, inw, back, small, ready):
    row = sum(jnp.pad(v, (AT[n], LANES - AT[n] - CUTS[n])) for n, v in zip(NAMES, small))[None]
    keep, send = pack(place, qkv, out, inw, back, row)
    pair = jnp.concatenate([keep, swap(send)], axis=0)
    one, two, rest = tile(place, spread_along(pair, "z"))
    rest = lax.all_gather(rest, ("x", "y", "c"), tiled=False).reshape(16, 2, 1296, LANES)
    one, two = line(place, spread_along(one, "x") + spread_along(two, "y"))
    parts, ready = together(spread_along(one, "y") + spread_along(two, "x"), ready)
    own = plane(place, parts)
    return own, swap(own), rest, ready


def held_columns(ref, block):
    rows = pl.ds(pl.multiple_of(48 * block, 16), 48)
    return ref[:, rows, :].reshape(D, LANES)


def columns(ref, count, height=48, halves=(0,)):
    rows = ref.shape[0] * height
    parts = [
        ref[:, half, height * j : height * (j + 1), :].reshape(rows, LANES)
        for half in halves
        for j in range(count)
    ]
    return parts[0] if len(parts) == 1 else jnp.concatenate(parts, axis=1)


OUT = pl.BlockSpec(
    (16, 2, 144, LANES), lambda *_: (0, 0, 8, 0), pipeline_mode=pl.Buffered(1)
)
HALF_STEPS = FF // STEP // 2
IN = pl.BlockSpec(
    (16, 1, STEP * 3 // 8, LANES), lambda b: (0, b // HALF_STEPS, b % HALF_STEPS, 0)
)
BACK = pl.BlockSpec((STEP // 192, 2, 576, LANES), lambda b: (b, 0, 1, 0))
ANYWHERE = pl.BlockSpec(memory_space=pl.ANY)
PAIR = pl.BlockSpec((ROWS, LANES), lambda p, *_: (0, p))
WIDE = pl.BlockSpec((ROWS, STEP), lambda b: (0, b))


def place_of(cut, shape_, dim):
    at = lax.broadcasted_iota(jnp.int32, shape_, dim)
    owner = (at * (10923 if cut == 6 else 2731)) >> 16
    return owner, at - owner * cut


def spread(rows, name):
    cut = CUTS[name]
    width = cut * 128
    _, place = place_of(cut, (LANES, width), 1)
    pick = lax.broadcasted_iota(jnp.int32, (LANES, width), 0) == place + AT[name]
    every = mul(rows, jnp.where(pick, 1.0, 0.0).astype(bf16))
    owner, _ = place_of(cut, (128, width), 1)
    here = lax.broadcasted_iota(jnp.int32, (128, width), 0) == owner
    return jnp.sum(jnp.where(here, every, 0.0), axis=0, keepdims=True)


def gathered_rows(vectors):
    total = jnp.zeros((128, LANES), f32)
    for name, vector in vectors:
        cut = CUTS[name]
        width = cut * 128
        owner, _ = place_of(cut, (128, width), 1)
        here = lax.broadcasted_iota(jnp.int32, (128, width), 0) == owner
        _, place = place_of(cut, (width, LANES), 0)
        pick = lax.broadcasted_iota(jnp.int32, (width, LANES), 1) == place + AT[name]
        own = jnp.where(here, vector, 0.0).astype(bf16)
        total = total + mul(own, jnp.where(pick, 1.0, 0.0).astype(bf16))
    total = total.reshape(16, 8, LANES)
    return jnp.concatenate([total, jnp.zeros((16, 8, LANES), f32)], axis=1).astype(bf16)


def normalise(total):
    centred = total - jnp.mean(total, axis=-1, keepdims=True)
    inverse = lax.rsqrt(jnp.mean(centred * centred, axis=-1, keepdims=True) + EPSILON)
    return centred * inverse, inverse


def norm_back(grad, normed, inverse, gain):
    scaled = grad * gain
    mean = jnp.mean(scaled, axis=-1, keepdims=True)
    slope = jnp.mean(scaled * normed, axis=-1, keepdims=True)
    return inverse * (scaled - mean - normed * slope)


def column_sum(value):
    return jnp.sum(value, axis=0, keepdims=True)


def head_mask(head):
    lane = lax.broadcasted_iota(jnp.int32, (ROWS, LANES), 1)
    return (lane < 64) if head == 0 else (lane >= 64)


def masked(value, head, factor=1.0):
    return jnp.where(head_mask(head), value.astype(f32) * factor, 0.0).astype(bf16)


def attend_kernel(
    place, x, sc, sr, own, other, q_o, k_o, v_o, lse_o, ctx_o, turn_o, vec_o, bin_o, bias, held,
    arrived_s,
):
    p = pl.program_id(0)

    @pl.when(p == 0)
    def _():
        core = place[3]
        copies = [
            pltpu.make_async_copy(own, held.at[core], arrived_s.at[0]),
            pltpu.make_async_copy(other, held.at[1 - core], arrived_s.at[1]),
        ]
        for copy in copies:
            copy.start()
        bias[...] = jnp.where(sc[...] == sr[...], 0.0, MASK_FILL)
        for copy in copies:
            copy.wait()
        rows = held[0, :, 432:448, :].astype(f32)[:, :8, :].reshape(128, LANES).astype(bf16)
        for name, row in ROW_OF.items():
            vec_o[row : row + 1, :] = spread(rows, name)
        bin_o[0:1, :] = spread(rows, "bi")

    weights = [held_columns(held.at[p // 3], 3 * t + p % 3) for t in range(3)]
    mixed = mul(x[...], jnp.concatenate(weights, axis=1))
    lanes = pl.ds(pl.multiple_of(p * LANES, LANES), LANES)
    q = (mixed[:, :LANES] + vec_o[0:1, lanes]).astype(bf16)
    k = mixed[:, LANES : 2 * LANES].astype(bf16)
    value = (mixed[:, 2 * LANES :] + vec_o[1:2, lanes]).astype(bf16)
    q_o[...], k_o[...], v_o[...] = q, k, value
    turned = value.astype(f32).T.astype(bf16)
    parts = []
    for head in range(2):
        scores = mul(k, masked(q, head, SCALE), LAST) + bias[...]
        top = jnp.max(scores, axis=0, keepdims=True)
        raised = jnp.exp(scores - top)
        total = jnp.sum(raised, axis=0, keepdims=True)
        lse_o[0, head : head + 1, :] = top + jnp.log(total)
        probs = (raised * (1.0 / total)).astype(bf16)
        parts.append(mul(turned[64 * head : 64 * (head + 1)], probs))
    context = jnp.concatenate(parts, axis=0)
    turn_o[...], ctx_o[...] = context.astype(bf16), context.T.astype(bf16)


def attend(place, x, seg_col, seg_row, own, other):
    wide, tall, pair = shape((ROWS, D), bf16), shape((D, ROWS), bf16), PAIR
    return run(
        attend_kernel,
        (6,),
        [whole((ROWS, D)), whole((ROWS, 1)), whole((1, ROWS)), ANYWHERE, ANYWHERE],
        [pair, pair, pair, pl.BlockSpec((1, 8, ROWS), lambda p, *_: (p, 0, 0)), pair]
        + [pl.BlockSpec((LANES, ROWS), lambda p, *_: (p, 0)), kept((8, D)), kept((8, FF))],
        [wide, wide, wide, shape((6, 8, ROWS)), wide, tall, shape((8, D)), shape((8, FF))],
        [pltpu.VMEM((ROWS, ROWS), f32), pltpu.VMEM((2, 16, 448, LANES), bf16)]
        + [pltpu.SemaphoreType.DMA((2,))],
        scalars=1,
        flops=6_000_000_000,
        size=12_000_000,
    )(place, x, seg_col, seg_row, own, other)


def forward_kernel(
    x, ctx, sc, cot, vec, bi, wi, wb, wo, act_o, slope_o, out_o, dsec_o, dbr_o, sums_o, n1_o, low_o,
    turn_o, inv_o, acc,
):
    b = pl.program_id(0)

    @pl.when(b == 0)
    def _():
        attn = mul(ctx[...], columns(wo, 3, halves=(0, 1))) + vec[2:3, :]
        normed, inverse = normalise(x[...].astype(f32) + attn)
        n1_o[...], inv_o[...] = normed, inverse
        first = normed * vec[3:4, :] + vec[4:5, :]
        low_o[...], turn_o[...] = first.astype(bf16), first.T.astype(bf16)

    pre = mul(low_o[...], columns(wi, STEP // LANES)) + bi[0:1, :]
    share = 0.5 * lax.erf(pre * 0.7071067811865476) + 0.5
    act = pre * share
    act_o[...] = act.T.astype(bf16)
    act = act.astype(bf16)
    slope_o[...] = (share + pre * (jnp.exp(pre * pre * -0.5) * 0.3989422804014327)).astype(bf16)
    term = mul(act, columns(wb, 3, 192, (0, 1)))

    @pl.when(b == 0)
    def _():
        acc[...] = term

    @pl.when(b > 0)
    def _():
        acc[...] += term

    @pl.when(b == FF // STEP - 1)
    def _():
        first = n1_o[...] * vec[3:4, :] + vec[4:5, :]
        normed, inverse = normalise(first + (acc[...] + vec[5:6, :]))
        valid = jnp.where(sc[...] > 0, 1.0, 0.0)
        out_o[...] = ((normed * vec[6:7, :] + vec[7:8, :]) * valid).astype(bf16)
        grad = cot[...].astype(f32) * valid
        sums_o[0:1, :] = column_sum(grad * normed)
        sums_o[1:2, :] = column_sum(grad)
        second = norm_back(grad, normed, inverse, vec[6:7, :])
        dsec_o[...] = second
        rounded = second.astype(bf16)
        dbr_o[...] = rounded
        sums_o[2:3, :] = column_sum(rounded.astype(f32))


def forward(x, ctx, seg_col, cot, vec, bi, gathered):
    deep, wide = shape((ROWS, FF), bf16), shape((ROWS, D), bf16)
    flat, out, sums = whole((ROWS, D)), kept((ROWS, D)), kept((8, D))
    return run(
        forward_kernel,
        (FF // STEP,),
        [flat, flat, whole((ROWS, 1)), flat, whole((8, D))]
        + [pl.BlockSpec((8, STEP), lambda b: (0, b)), IN, BACK, OUT],
        [pl.BlockSpec((STEP, ROWS), lambda b: (b, 0)), WIDE, out, out, out, sums]
        + [out, out, kept((D, ROWS)), kept((ROWS, 1))],
        [shape((FF, ROWS), bf16), deep, wide, shape((ROWS, D)), wide, shape((8, D))]
        + [shape((ROWS, D)), wide, shape((D, ROWS), bf16), shape((ROWS, 1))],
        [pltpu.VMEM((ROWS, D), f32)],
        flops=10_000_000_000,
        size=20_000_000,
    )(x, ctx, seg_col, cot, vec, bi, gathered, gathered, gathered)


def backward_one_kernel(dbr, slope, dsec, wi, wb, dpre_o, bi_o, acc):
    b = pl.program_id(0)
    dact = mul(dbr[...], columns(wb, 3, 192, (0, 1)), LAST)
    dpre = (dact * slope[...].astype(f32)).astype(bf16)
    dpre_o[...] = dpre
    bi_o[0:1, :] = column_sum(dpre.astype(f32))
    term = mul(dpre, columns(wi, STEP // LANES), LAST)

    @pl.when(b == 0)
    def _():
        acc[...] = dsec[...] + term

    @pl.when(b > 0)
    def _():
        acc[...] += term


def backward_two_kernel(
    dbr, slope, dsec, wi, wb, wo, n1, inv, vec, dpre_in, bi_in, dpre_o, bi_o, dfirst_o, dattn_o,
    dctx_o, sums_o, acc,
):
    backward_one_kernel(dbr, slope, dsec, wi, wb, dpre_o, bi_o, acc)

    @pl.when(pl.program_id(0) == HALF_STEPS - 1)
    def _():
        grad, normed = acc[...], n1[...]
        sums_o[0:1, :] = column_sum(grad * normed)
        sums_o[1:2, :] = column_sum(grad)
        first = norm_back(grad, normed, inv[...], vec[3:4, :])
        dfirst_o[...] = first
        rounded = first.astype(bf16)
        dattn_o[...] = rounded
        sums_o[2:3, :] = column_sum(rounded.astype(f32))
        dctx_o[...] = mul(rounded, columns(wo, 3, halves=(0, 1)), LAST).astype(bf16)


def backward_specs(half):
    first = HALF_STEPS * half
    ins = [
        whole((ROWS, D)),
        pl.BlockSpec((ROWS, STEP), lambda b: (0, first + b)),
        whole((ROWS, D)),
        pl.BlockSpec((16, 1, STEP * 3 // 8, LANES), lambda b: (0, half, b, 0)),
        pl.BlockSpec((STEP // 192, 2, 576, LANES), lambda b: (first + b, 0, 1, 0)),
    ]
    outs = [
        pl.BlockSpec((ROWS, STEP), lambda b: (0, first + b)),
        pl.BlockSpec((8, STEP), lambda b: (0, first + b)),
    ]
    return ins, outs, [shape((ROWS, FF), bf16), shape((8, FF))]


def backward_one(dbr, slope, dsec, gathered):
    ins, outs, shapes = backward_specs(0)
    return run(
        backward_one_kernel,
        (HALF_STEPS,),
        ins,
        outs + [kept((ROWS, D))],
        shapes + [shape((ROWS, D))],
        flops=5_000_000_000,
        size=10_000_000,
    )(dbr, slope, dsec, gathered, gathered)


def backward_two(dbr, slope, acc, n1, inv, vec, dpre, bi, gathered):
    wide, flat = shape((ROWS, D), bf16), whole((ROWS, D))
    ins, outs, shapes = backward_specs(1)
    return run(
        backward_two_kernel,
        (HALF_STEPS,),
        ins + [OUT, flat, whole((ROWS, 1)), whole((8, D)), ANYWHERE, ANYWHERE],
        outs + [kept((ROWS, D)), kept((ROWS, D)), kept((ROWS, D)), kept((8, D))],
        shapes + [shape((ROWS, D)), wide, wide, shape((8, D))],
        [pltpu.VMEM((ROWS, D), f32)],
        flops=6_000_000_000,
        size=10_000_000,
        alias={9: 0, 10: 1},
    )(dbr, slope, acc, gathered, gathered, gathered, n1, inv, vec, dpre, bi)


def attend_back_kernel(
    half, place, q, k, v, dctx, lse, sc, sr, dfirst, own, other, mixed_o, sums_o, dx_o, bias, acc,
    held, arrived_s,
):
    p = pl.program_id(0)

    @pl.when(p == 0)
    def _():
        bias[...] = jnp.where(sc[...] == sr[...], 0.0, MASK_FILL)
        acc[...] = dfirst[...]
        for here, source in ((half, own), (1 - half, other)):

            @pl.when(place[3] == here)
            def _():
                copy = pltpu.make_async_copy(source.at[:, :432, :], held, arrived_s.at[0])
                copy.start()
                copy.wait()

    key, value = k[...], v[...]
    turned = key.astype(f32).T.astype(bf16)
    dk = jnp.zeros((ROWS, LANES), f32)
    dv = jnp.zeros((ROWS, LANES), f32)
    parts = []
    for head in range(2):
        query = masked(q[...], head, SCALE)
        grad = masked(dctx[...], head)
        probs = jnp.exp(mul(key, query, LAST) + bias[...] - lse[0, head : head + 1, :])
        dprobs = mul(value, grad, LAST)
        dv = dv + mul(probs.astype(bf16), grad)
        dscores = (probs * (dprobs - column_sum(probs * dprobs))).astype(bf16)
        dk = dk + mul(dscores, query)
        parts.append(mul(turned[64 * head : 64 * (head + 1)], dscores))
    dq = (jnp.concatenate(parts, axis=0).T * SCALE).astype(bf16)
    dk, dv = dk.astype(bf16), dv.astype(bf16)
    mixed_o[0], mixed_o[1], mixed_o[2] = dq, dk, dv
    sums_o[0:1, :] = column_sum(dq.astype(f32))
    sums_o[1:2, :] = column_sum(dv.astype(f32))
    weight = jnp.concatenate([held_columns(held, 3 * t + p) for t in range(3)], axis=1)
    acc[...] += mul(jnp.concatenate([dq, dk, dv], axis=1), weight, LAST)

    @pl.when(p == 2)
    def _():
        dx_o[...] = acc[...].astype(dx_o.dtype)


def attend_back(half, place, q, k, v, dctx, lse, seg_col, seg_row, dfirst, own, other):
    pair = pl.BlockSpec((ROWS, LANES), lambda p, *_: (0, 3 * half + p))
    return run(
        functools.partial(attend_back_kernel, half),
        (3,),
        [pair, pair, pair, pair, pl.BlockSpec((1, 8, ROWS), lambda p, *_: (3 * half + p, 0, 0))]
        + [whole((ROWS, 1)), whole((1, ROWS)), whole((ROWS, D)), ANYWHERE, ANYWHERE],
        [pl.BlockSpec((3, ROWS, LANES), lambda p, *_: (0, 0, p))]
        + [pl.BlockSpec((8, LANES), lambda p, *_: (0, p)), kept((ROWS, D))],
        [shape((3, ROWS, 384), bf16), shape((8, 384)), shape((ROWS, D), (f32, bf16)[half])],
        [pltpu.VMEM((ROWS, ROWS), f32), pltpu.VMEM((ROWS, D), f32)]
        + [pltpu.VMEM((16, 432, LANES), bf16), pltpu.SemaphoreType.DMA((1,))],
        scalars=1,
        flops=6_000_000_000,
        size=8_000_000,
    )(place, q, k, v, dctx, lse, seg_col, seg_row, dfirst, own, other)


def put(total, at, grad):
    rows = grad.astype(bf16).reshape(16, 48, -1)
    for j in range(rows.shape[2] // LANES):
        total[:, pl.ds(at + 48 * j, 48), :] = rows[:, :, LANES * j : LANES * (j + 1)]


def back_grad_kernel(place, act, act_2, dbr, dbr_2, total):
    grad = (mul(act[...], dbr[...]) + mul(act_2[...], dbr_2[...])).astype(bf16)
    for at in range(2):
        for j in range(3):
            part = grad[192 * at : 192 * (at + 1), LANES * j : LANES * (j + 1)]
            total[at, 192 * j : 192 * (j + 1), :] = part

def back_grad(place, act, act_2, dbr, dbr_2):
    tall = pl.BlockSpec((384, ROWS), lambda b, p: (b, 0))
    half = pl.BlockSpec((ROWS, 384), lambda b, p: (0, p[3]))
    return run(
        back_grad_kernel,
        (8,),
        [tall, tall, half, half],
        pl.BlockSpec((2, 576, LANES), lambda b, p: (b, 0, 0)),
        shape((16, 576, LANES), bf16),
        scalars=1,
        flops=2_400_000_000,
        size=10_000_000,
    )(place, act, act_2, dbr, dbr_2)


def middle_grad_kernel(
    place, low, low_2, dpre, dpre_2, ctx, ctx_2, dattn, dattn_2, two, bi, one, total
):
    b = pl.program_id(0)

    @pl.when(b < 4)
    def _():
        grad = mul(low[...], dpre[...]) + mul(low_2[...], dpre_2[...])
        put(total, pl.multiple_of(144 * b, 16), grad)

    @pl.when(b == 4)
    def _():
        put(total, 576, mul(ctx[...], dattn[...]) + mul(ctx_2[...], dattn_2[...]))
        names = (("g2", two, 0), ("s2", two, 1), ("bb", two, 2), ("bi", bi, 0))
        names = names + (("g1", one, 0), ("s1", one, 1), ("bo", one, 2))
        total[:, 720:736, :] = gathered_rows([(n, ref[i : i + 1, :]) for n, ref, i in names])


def middle_grad(place, low, low_2, dpre, dpre_2, ctx, ctx_2, dattn, dattn_2, two, bi, one):
    tall = whole((D, ROWS))
    quarter = pl.BlockSpec((ROWS, 384), lambda b, p: (0, 4 * p[3] + jnp.minimum(b, 3)))
    half = pl.BlockSpec((ROWS, 384), lambda b, p: (0, p[3]))
    return run(
        middle_grad_kernel,
        (5,),
        [tall, tall, quarter, quarter, tall, tall, half, half]
        + [whole((8, D)), whole((8, FF)), whole((8, D))],
        kept((16, 736, LANES)),
        shape((16, 736, LANES), bf16),
        scalars=1,
        flops=3_200_000_000,
        size=12_000_000,
    )(place, low, low_2, dpre, dpre_2, ctx, ctx_2, dattn, dattn_2, two, bi, one)


def qkv_grad_kernel(place, x, x_2, left, left_2, right, right_2, sums_l, sums_r, total):
    for core, own, other in ((0, left, left_2), (1, right, right_2)):

        @pl.when(place[3] == core)
        def _():
            for t in range(3):
                put(total, 144 * t, mul(x[...], own[t]) + mul(x_2[...], other[t]))

    sums = [jnp.concatenate([sums_l[i : i + 1, :], sums_r[i : i + 1, :]], axis=1) for i in (0, 1)]
    total[:, 432:448, :] = gathered_rows([("bq", sums[0]), ("bv", sums[1])])


def qkv_grad(place, x, x_2, left, left_2, right, right_2, sums_l, sums_r):
    half = kept((3, ROWS, 384))
    return run(
        qkv_grad_kernel,
        (1,),
        [kept((D, ROWS)), kept((D, ROWS)), half, half, half, half, kept((8, 384)), kept((8, 384))],
        kept((16, 448, LANES)),
        shape((16, 448, LANES), bf16),
        scalars=1,
        flops=1_800_000_000,
        size=7_000_000,
    )(place, x, x_2, left, left_2, right, right_2, sums_l, sums_r)


def last_kernel(place, *refs):
    early, late, outs = refs[0], refs[1], refs[2:]
    back, middle = early[:576, :].astype(f32), early[576:, :].astype(f32)
    qkv = late[0].astype(f32)
    for i in range(1, 16):
        qkv = qkv + late[i].astype(f32)
    wide = [qkv[48 * j : 48 * (j + 1)] for j in range(9)]
    wide = wide + [middle[576 + 48 * j : 576 + 48 * (j + 1)] for j in range(3)]
    wide = wide + [middle[48 * j : 48 * (j + 1)] for j in range(12)]
    rows = middle[720:728] + qkv[432:440]
    none = jnp.zeros((4, LANES), f32)
    for z in range(4):
        parts = []
        for block in wide:
            parts = parts + [block[12 * z : 12 * (z + 1)], none]
        for j in range(3):
            parts.append(back[192 * j + 48 * z : 192 * j + 48 * (z + 1)])
        parts = parts + [rows[2 * z : 2 * (z + 1)], jnp.zeros((14, LANES), f32)]
        total = jnp.concatenate(parts, axis=0).astype(bf16)
        for k in range(4):

            @pl.when((place[2] + k) % 4 == z)
            def _():
                outs[k][...] = total


def last_sum(place, parts):
    return run(
        last_kernel,
        (1,),
        [kept(p.shape) for p in parts],
        [kept((544, LANES))] * 4,
        [shape((544, LANES), bf16)] * 4,
        scalars=1,
        size=4_000_000,
    )(place, *parts)


def around(parts, axis):
    return [parts[0]] + [lax.ppermute(parts[k], axis, shifted(4, k)) for k in (1, 3, 2)]


def scattered(value, axis):
    return lax.psum_scatter(value, axis, tiled=True)


def swap(value):
    return lax.ppermute(value, "c", shifted(2, 1))


def together(*values):
    flat, tree = jax.tree.flatten(values)
    return jax.tree.unflatten(tree, lax.optimization_barrier(tuple(flat)))


def assemble_kernel(place, own, other, qkv, out, inw, back, row):
    mine, theirs = own[...], other[...].astype(f32)
    row[...] = mine[216:217] + theirs[216:217]
    for core in range(2):

        @pl.when(place[3] == core)
        def _():
            for half, rows in ((core, mine), (1 - core, theirs)):
                blocks = [(qkv, 6 * t + 3 * half + j) for t in range(3) for j in range(3)]
                blocks += [(out, 3 * half + j) for j in range(3)]
                blocks += [(inw, 12 * half + j) for j in range(12)]
                for i, (ref, j) in enumerate(blocks):
                    ref[:, LANES * j : LANES * (j + 1)] = rows[6 * i : 6 * (i + 1)]
                for i in range(3):
                    j = 3 * half + i
                    part = rows[144 + 24 * i : 144 + 24 * (i + 1)]
                    back[:, LANES * j : LANES * (j + 1)] = part


def assemble(place, own, other):
    outs = [(6, 3 * D), (6, D), (6, FF), (24, D), (1, LANES)]
    return run(
        assemble_kernel,
        (1,),
        [kept((224, LANES))] * 2,
        [kept(o) for o in outs],
        [shape(o) for o in outs],
        scalars=1,
    )(place, own, other)


def finish(place, core, parts):
    parts = around(last_sum(place, parts), "z")
    total = sum(p.astype(f32) for p in parts)
    wide = total[:384].reshape(24, 16, LANES)[:, :12].reshape(24, 2, 6, LANES)
    tall = total[384:528].reshape(3, 2, 24, LANES)

    def for_core(which):
        a = lax.dynamic_index_in_dim(wide, which, 1, keepdims=False).reshape(144, LANES)
        b = lax.dynamic_index_in_dim(tall, which, 1, keepdims=False).reshape(72, LANES)
        row = lax.dynamic_index_in_dim(total[528:530], which, 0)
        return jnp.concatenate([a, b, row, jnp.zeros((7, LANES), f32)], axis=0)

    own = for_core(core)
    other = swap(for_core(1 - core).astype(bf16))
    *weights, rows = assemble(place, own, other)
    return weights, {n: rows[0, AT[n] : AT[n] + CUTS[n]] for n in NAMES}


def segment_rows(lengths, assignment, device, rows):
    count = lengths.shape[0]
    order = jnp.arange(count, dtype=jnp.int32)
    same = assignment[:, None] == assignment[None, :]
    before = order[None, :] < order[:, None]
    offset = jnp.sum(jnp.where(same & before, lengths[None, :], 0), axis=1)
    places = jnp.arange(rows, dtype=jnp.int32)[:, None]
    inside = (
        (assignment[None, :] == device)
        & (places >= offset[None, :])
        & (places < (offset + lengths)[None, :])
    )
    return jnp.sum(jnp.where(inside, order[None, :] + 1, 0), axis=1)


def body(
    hidden_in,
    out_cotangent,
    lengths,
    assignment,
    qkv_weight,
    query_bias,
    value_bias,
    out_weight,
    out_bias,
    first_gain,
    first_shift,
    in_weight,
    in_bias,
    back_weight,
    back_bias,
    second_gain,
    second_shift,
):
    small = [
        query_bias,
        value_bias,
        out_bias,
        first_gain,
        first_shift,
        in_bias,
        back_bias,
        second_gain,
        second_shift,
    ]
    px, py, pz, core = (lax.axis_index(a) for a in ("x", "y", "z", "c"))
    place = jnp.stack([px, py, pz, core]).astype(jnp.int32)
    segment = segment_rows(lengths, assignment, ((px * 4 + py) * 4 + pz) * 2 + core, ROWS)
    seg_col, seg_row = segment.reshape(ROWS, 1), segment.reshape(1, ROWS)
    ready = (hidden_in.T, seg_col, seg_row)
    own, other, gathered, ready = gather_all(
        place, qkv_weight, out_weight, in_weight, back_weight, small, ready
    )
    turned, seg_col, seg_row = ready
    q, k, v, lse, ctx_rows, ctx, vec, bi = attend(
        place, hidden_in, seg_col, seg_row, own, other
    )
    turned_2, ctx_2 = swap(turned), swap(ctx)
    act, slope, layer_out, dsec, dbr, two, n1, low, low_t, inv = forward(
        hidden_in, ctx_rows, seg_col, out_cotangent, vec, bi, gathered
    )
    act, dbr, turned_2, ctx_2 = together(act, dbr, turned_2, ctx_2)
    act_2, dbr_2, low_2 = swap(act), swap(dbr), swap(low_t)
    dpre, dbi, acc = backward_one(dbr, slope, dsec, gathered)
    act_2, dbr_2, low_2, acc = together(act_2, dbr_2, low_2, acc)
    back = back_grad(place, act, act_2, dbr, dbr_2)
    back, acc = together(back, acc)
    back = scattered(back.reshape(-1, LANES), "x")
    dpre, dbi, dfirst, dattn, dctx, one = backward_two(
        dbr, slope, acc, n1, inv, vec, dpre, dbi, gathered
    )
    dpre_2, dattn_2 = swap(dpre), swap(dattn)
    middle = middle_grad(
        place, low_t, low_2, dpre, dpre_2, ctx, ctx_2, dattn, dattn_2, two, dbi, one
    )
    middle, dctx = together(middle, dctx)
    middle = scattered(middle.reshape(-1, LANES), "x")
    left, sums_l, acc = attend_back(
        0, place, q, k, v, dctx, lse, seg_col, seg_row, dfirst, own, other
    )
    left_2 = swap(left)
    right, sums_r, input_grad = attend_back(
        1, place, q, k, v, dctx, lse, seg_col, seg_row, acc, own, other
    )
    left_2, right = together(left_2, right)
    right_2 = swap(right)
    late = qkv_grad(place, turned, turned_2, left, left_2, right, right_2, sums_l, sums_r)
    back, middle, late = together(back, middle, late)
    early = [back.reshape(4, 576, LANES), middle.reshape(4, 736, LANES)]
    early, late = together(jnp.concatenate(early, axis=1).reshape(-1, LANES), late)
    parts = [scattered(early, "y"), lax.all_to_all(late, ("x", "y"), 0, 0, tiled=True)]
    weights, s = finish(place, core, parts)
    return (
        layer_out,
        input_grad,
        weights[0],
        s["bq"],
        s["bv"],
        weights[1],
        s["bo"],
        s["g1"],
        s["s1"],
        weights[2],
        s["bi"],
        weights[3],
        s["bb"],
        s["g2"],
        s["s2"],
    )


def solution(mesh):
    axes = ("x", "y", "z", "c")
    grid = Mesh(mesh.devices.reshape(4, 4, 4, 2), axes)
    two, one, every = P(axes, None), P(axes), P()
    in_specs = (two, two, every, every, two, one, one, two, one, one, one, two, one, two)
    in_specs = in_specs + (one, one, one)
    out_specs = (two, two, two, one, one, two, one, one, one, two, one, two, one, one, one)
    return jax.shard_map(body, mesh=grid, in_specs=in_specs, out_specs=out_specs, check_vma=False)
```

```python
import functools

import jax
import jax.numpy as jnp
from jax import lax
from jax.experimental import pallas as pl
from jax.experimental.pallas import tpu as pltpu
from jax.sharding import Mesh, PartitionSpec as P

ROWS = 512
STEP = 768
D = 768
FF = 3072
LANES = 128
EPSILON = 1e-05
SCALE = 0.125
MASK_FILL = -1000000000.0
bf16, f32 = jnp.bfloat16, jnp.float32
NAMES = ("bq", "bv", "bo", "g1", "s1", "bi", "bb", "g2", "s2")
CUTS = dict(zip(NAMES, (6, 6, 6, 6, 6, 24, 6, 6, 6)))
AT = dict(zip(NAMES, (0, 6, 12, 18, 24, 30, 54, 60, 66)))
ROW_OF = dict(bq=0, bv=1, bo=2, g1=3, s1=4, bb=5, g2=6, s2=7)
LAST = (((1,), (1,)), ((), ()))
FIRST = (((0,), (0,)), ((), ()))


def shape(dims, kind=f32):
    return jax.ShapeDtypeStruct(dims, kind)


def whole(dims):
    return pl.BlockSpec(dims, lambda *_: (0,) * len(dims), pipeline_mode=pl.Buffered(1))


def kept(dims):
    return pl.BlockSpec(dims, lambda *_: (0,) * len(dims))


def run(kernel, grid, ins, outs, shapes, scratch=(), scalars=0, flops=0, size=0, alias=None):
    return pl.pallas_call(
        kernel,
        grid_spec=pltpu.PrefetchScalarGridSpec(
            num_scalar_prefetch=scalars,
            grid=grid,
            in_specs=ins,
            out_specs=outs,
            scratch_shapes=scratch,
        ),
        out_shape=shapes,
        input_output_aliases=alias or {},
        compiler_params=pltpu.CompilerParams(vmem_limit_bytes=64 * 1024 * 1024),
        cost_estimate=pl.CostEstimate(flops=flops, bytes_accessed=size, transcendentals=0),
    )


def mul(a, b, dims=(((1,), (0,)), ((), ()))):
    return lax.dot_general(a, b, dims, preferred_element_type=f32)


def shifted(n, step):
    return [(i, (i + step) % n) for i in range(n)]


def pack_kernel(place, qkv, out, inw, back, row, keep_o, send_o):
    halves = []
    for half in range(2):
        blocks = [(qkv, 6 * t + 3 * half + j) for t in range(3) for j in range(3)]
        blocks += [(out, 3 * half + j) for j in range(3)]
        blocks += [(inw, 12 * half + j) for j in range(12)]
        blocks += [(back, 3 * half + j) for j in range(3)]
        parts = [ref[:, LANES * j : LANES * (j + 1)].astype(f32) for ref, j in blocks]
        parts += [row[...].astype(f32), jnp.zeros((7, LANES), f32)]
        halves.append(jnp.concatenate(parts, axis=0).astype(bf16))
    for core in range(2):

        @pl.when(place[3] == core)
        def _():
            keep_o[...], send_o[...] = halves[core], halves[1 - core]


def pack(place, qkv, out, inw, back, row):
    arrays = (qkv, out, inw, back, row)
    return run(
        pack_kernel,
        (1,),
        [kept(a.shape) for a in arrays],
        [kept((224, LANES))] * 2,
        [shape((224, LANES), bf16)] * 2,
        scalars=1,
    )(place, *arrays)


def tile_kernel(place, *refs):
    ins, (one_o, two_o, rest_o, near) = refs[:4], refs[4:]
    core = place[3]
    for ref, k in zip(ins, (0, 1, 3, 2)):
        z = (place[2] + 4 - k) % 4
        near[z, core] = ref[:224, :].astype(f32)
        near[z, 1 - core] = ref[224:, :].astype(f32)

    def block(first, height):
        parts = [near[z, c, first : first + height, :] for z in range(4) for c in range(2)]
        return jnp.concatenate(parts, axis=0)

    head = [block(6 * i, 6) for i in range(9)] + [block(216, 1), jnp.zeros((8, LANES), f32)]
    head = jnp.concatenate(head, axis=0).astype(bf16)
    one_o[...], two_o[...] = head[:224], head[224:]
    rest = [block(6 * i, 6) for i in range(12, 24)] + [block(144 + 24 * j, 24) for j in range(3)]
    rest = rest + [block(6 * i, 6) for i in range(9, 12)]
    rest_o[...] = jnp.concatenate(rest, axis=0).astype(bf16)


def tile(place, parts):
    return run(
        tile_kernel,
        (1,),
        [kept((448, LANES))] * 4,
        [kept((224, LANES)), kept((224, LANES)), kept((1296, LANES))],
        [shape((224, LANES), bf16), shape((224, LANES), bf16), shape((1296, LANES), bf16)],
        [pltpu.VMEM((4, 2, 224, LANES), f32)],
        scalars=1,
    )(place, *parts)


def line_kernel(place, *refs):
    ins, outs = refs[:8], refs[8:]
    for out, first, at in ((outs[0], 0, place[0]), (outs[1], 4, place[1])):
        for i, k in enumerate((0, 1, 3, 2)):
            out[(at + 4 - k) % 4] = ins[first + i][...]


def line(place, parts):
    outs = [(4, *parts[0].shape), (4, *parts[4].shape)]
    return run(
        line_kernel,
        (1,),
        [kept(p.shape) for p in parts],
        [kept(o) for o in outs],
        [shape(o, bf16) for o in outs],
        scalars=1,
    )(place, *parts)


def plane_kernel(place, *refs):
    ins, out = refs[:8], refs[8]
    rows = ins[0].shape[1]
    for i, k in enumerate((0, 1, 3, 2)):
        x, y = (place[0] + 4 - k) % 4, (place[1] + 4 - k) % 4
        for j in range(4):
            out[4 * j + y, :rows, :] = ins[i][j]
            out[4 * x + j, rows:, :] = ins[4 + i][j]


def plane(place, parts):
    rows = parts[0].shape[1] + parts[4].shape[1]
    return run(
        plane_kernel,
        (1,),
        [kept(p.shape) for p in parts],
        kept((16, rows, LANES)),
        shape((16, rows, LANES), bf16),
        scalars=1,
    )(place, *parts)


def spread_along(value, axis):
    return [value] + [lax.ppermute(value, axis, shifted(4, k)) for k in (1, 3, 2)]


def gather_all(place, qkv, out, inw, back, small, ready):
    row = sum(jnp.pad(v, (AT[n], LANES - AT[n] - CUTS[n])) for n, v in zip(NAMES, small))[None]
    keep, send = pack(place, qkv, out, inw, back, row)
    pair = jnp.concatenate([keep, swap(send)], axis=0)
    one, two, rest = tile(place, spread_along(pair, "z"))
    rest = lax.all_gather(rest, ("x", "y", "c"), tiled=False).reshape(16, 2, 1296, LANES)
    one, two = line(place, spread_along(one, "x") + spread_along(two, "y"))
    parts, ready = together(spread_along(one, "y") + spread_along(two, "x"), ready)
    own = plane(place, parts)
    return own, swap(own), rest, ready


def held_columns(ref, block):
    rows = pl.ds(pl.multiple_of(48 * block, 16), 48)
    return ref[:, rows, :].reshape(D, LANES)


def columns(ref, count, height=48, halves=(0,)):
    rows = ref.shape[0] * height
    parts = [
        ref[:, half, height * j : height * (j + 1), :].reshape(rows, LANES)
        for half in halves
        for j in range(count)
    ]
    return parts[0] if len(parts) == 1 else jnp.concatenate(parts, axis=1)


OUT = pl.BlockSpec(
    (16, 2, 144, LANES), lambda *_: (0, 0, 8, 0), pipeline_mode=pl.Buffered(1)
)
HALF_STEPS = FF // STEP // 2
IN = pl.BlockSpec(
    (16, 1, STEP * 3 // 8, LANES), lambda b: (0, b // HALF_STEPS, b % HALF_STEPS, 0)
)
BACK = pl.BlockSpec((STEP // 192, 2, 576, LANES), lambda b: (b, 0, 1, 0))
ANYWHERE = pl.BlockSpec(memory_space=pl.ANY)
PAIR = pl.BlockSpec((ROWS, LANES), lambda p, *_: (0, p))
WIDE = pl.BlockSpec((ROWS, STEP), lambda b: (0, b))


def place_of(cut, shape_, dim):
    at = lax.broadcasted_iota(jnp.int32, shape_, dim)
    owner = (at * (10923 if cut == 6 else 2731)) >> 16
    return owner, at - owner * cut


def spread(rows, name):
    cut = CUTS[name]
    width = cut * 128
    _, place = place_of(cut, (LANES, width), 1)
    pick = lax.broadcasted_iota(jnp.int32, (LANES, width), 0) == place + AT[name]
    every = mul(rows, jnp.where(pick, 1.0, 0.0).astype(bf16))
    owner, _ = place_of(cut, (128, width), 1)
    here = lax.broadcasted_iota(jnp.int32, (128, width), 0) == owner
    return jnp.sum(jnp.where(here, every, 0.0), axis=0, keepdims=True)


def gathered_rows(vectors):
    total = jnp.zeros((128, LANES), f32)
    for name, vector in vectors:
        cut = CUTS[name]
        width = cut * 128
        owner, _ = place_of(cut, (128, width), 1)
        here = lax.broadcasted_iota(jnp.int32, (128, width), 0) == owner
        _, place = place_of(cut, (width, LANES), 0)
        pick = lax.broadcasted_iota(jnp.int32, (width, LANES), 1) == place + AT[name]
        own = jnp.where(here, vector, 0.0).astype(bf16)
        total = total + mul(own, jnp.where(pick, 1.0, 0.0).astype(bf16))
    total = total.reshape(16, 8, LANES)
    return jnp.concatenate([total, jnp.zeros((16, 8, LANES), f32)], axis=1).astype(bf16)


def normalise(total):
    centred = total - jnp.mean(total, axis=-1, keepdims=True)
    inverse = lax.rsqrt(jnp.mean(centred * centred, axis=-1, keepdims=True) + EPSILON)
    return centred * inverse, inverse


def norm_back(grad, normed, inverse, gain):
    scaled = grad * gain
    mean = jnp.mean(scaled, axis=-1, keepdims=True)
    slope = jnp.mean(scaled * normed, axis=-1, keepdims=True)
    return inverse * (scaled - mean - normed * slope)


def column_sum(value):
    return jnp.sum(value, axis=0, keepdims=True)


def upright(row):
    return jnp.broadcast_to(row.astype(f32), (8, ROWS)).T[:, 0:1]


def head_mask(head):
    lane = lax.broadcasted_iota(jnp.int32, (ROWS, LANES), 1)
    return (lane < 64) if head == 0 else (lane >= 64)


def masked(value, head, factor=1.0):
    return jnp.where(head_mask(head), value.astype(f32) * factor, 0.0).astype(bf16)


def attend_kernel(
    place, x, sr, own, other, q_o, k_o, v_o, lse_o, ctx_o, turn_o, vec_o, bin_o, bias, held,
    arrived_s,
):
    p = pl.program_id(0)

    @pl.when(p == 0)
    def _():
        core = place[3]
        copies = [
            pltpu.make_async_copy(own, held.at[core], arrived_s.at[0]),
            pltpu.make_async_copy(other, held.at[1 - core], arrived_s.at[1]),
        ]
        for copy in copies:
            copy.start()
        bias[...] = jnp.where(upright(sr[...]) == sr[...].astype(f32), 0.0, MASK_FILL)
        for copy in copies:
            copy.wait()
        rows = held[0, :, 432:448, :].astype(f32)[:, :8, :].reshape(128, LANES).astype(bf16)
        for name, row in ROW_OF.items():
            vec_o[row : row + 1, :] = spread(rows, name)
        bin_o[0:1, :] = spread(rows, "bi")

    weights = [held_columns(held.at[p // 3], 3 * t + p % 3) for t in range(3)]
    mixed = mul(x[...], jnp.concatenate(weights, axis=1))
    lanes = pl.ds(pl.multiple_of(p * LANES, LANES), LANES)
    q = (mixed[:, :LANES] + vec_o[0:1, lanes]).astype(bf16)
    k = mixed[:, LANES : 2 * LANES].astype(bf16)
    value = (mixed[:, 2 * LANES :] + vec_o[1:2, lanes]).astype(bf16)
    q_o[...], k_o[...], v_o[...] = q, k, value
    turned = value.astype(f32).T.astype(bf16)
    parts = []
    for head in range(2):
        scores = mul(k, masked(q, head, SCALE), LAST) + bias[...]
        top = jnp.max(scores, axis=0, keepdims=True)
        raised = jnp.exp(scores - top)
        total = jnp.sum(raised, axis=0, keepdims=True)
        lse_o[0, head : head + 1, :] = top + jnp.log(total)
        probs = (raised * (1.0 / total)).astype(bf16)
        parts.append(mul(turned[64 * head : 64 * (head + 1)], probs))
    context = jnp.concatenate(parts, axis=0)
    turn_o[...], ctx_o[...] = context.astype(bf16), context.T.astype(bf16)


def attend(place, x, seg_row, own, other):
    wide, tall, pair = shape((ROWS, D), bf16), shape((D, ROWS), bf16), PAIR
    return run(
        attend_kernel,
        (6,),
        [whole((ROWS, D)), whole((1, ROWS)), ANYWHERE, ANYWHERE],
        [pair, pair, pair, pl.BlockSpec((1, 8, ROWS), lambda p, *_: (p, 0, 0)), pair]
        + [pl.BlockSpec((LANES, ROWS), lambda p, *_: (p, 0)), kept((8, D)), kept((8, FF))],
        [wide, wide, wide, shape((6, 8, ROWS)), wide, tall, shape((8, D)), shape((8, FF))],
        [pltpu.VMEM((ROWS, ROWS), f32), pltpu.VMEM((2, 16, 448, LANES), bf16)]
        + [pltpu.SemaphoreType.DMA((2,))],
        scalars=1,
        flops=6_000_000_000,
        size=12_000_000,
    )(place, x, seg_row, own, other)


def forward_kernel(
    x, ctx, sr, cot, vec, bi, wi, wb, wo, act_o, slope_o, out_o, dsec_o, dbr_o, sums_o, n1_o, low_o,
    turn_o, inv_o, acc,
):
    b = pl.program_id(0)

    @pl.when(b == 0)
    def _():
        attn = mul(ctx[...], columns(wo, 3, halves=(0, 1))) + vec[2:3, :]
        normed, inverse = normalise(x[...].astype(f32) + attn)
        n1_o[...], inv_o[...] = normed, inverse
        first = normed * vec[3:4, :] + vec[4:5, :]
        low_o[...], turn_o[...] = first.astype(bf16), first.T.astype(bf16)

    pre = mul(low_o[...], columns(wi, STEP // LANES)) + bi[0:1, :]
    share = 0.5 * lax.erf(pre * 0.7071067811865476) + 0.5
    act = pre * share
    act_o[...] = act.T.astype(bf16)
    act = act.astype(bf16)
    slope_o[...] = (share + pre * (jnp.exp(pre * pre * -0.5) * 0.3989422804014327)).astype(bf16)
    term = mul(act, columns(wb, 3, 192, (0, 1)))

    @pl.when(b == 0)
    def _():
        acc[...] = term

    @pl.when(b > 0)
    def _():
        acc[...] += term

    @pl.when(b == FF // STEP - 1)
    def _():
        first = n1_o[...] * vec[3:4, :] + vec[4:5, :]
        normed, inverse = normalise(first + (acc[...] + vec[5:6, :]))
        valid = jnp.where(upright(sr[...]) > 0.0, 1.0, 0.0)
        out_o[...] = ((normed * vec[6:7, :] + vec[7:8, :]) * valid).astype(bf16)
        grad = cot[...].astype(f32) * valid
        sums_o[0:1, :] = column_sum(grad * normed)
        sums_o[1:2, :] = column_sum(grad)
        second = norm_back(grad, normed, inverse, vec[6:7, :])
        dsec_o[...] = second
        rounded = second.astype(bf16)
        dbr_o[...] = rounded
        sums_o[2:3, :] = column_sum(rounded.astype(f32))


def forward(x, ctx, seg_row, cot, vec, bi, gathered):
    deep, wide = shape((ROWS, FF), bf16), shape((ROWS, D), bf16)
    flat, out, sums = whole((ROWS, D)), kept((ROWS, D)), kept((8, D))
    return run(
        forward_kernel,
        (FF // STEP,),
        [flat, flat, whole((1, ROWS)), flat, whole((8, D))]
        + [pl.BlockSpec((8, STEP), lambda b: (0, b)), IN, BACK, OUT],
        [pl.BlockSpec((STEP, ROWS), lambda b: (b, 0)), WIDE, out, out, out, sums]
        + [out, out, kept((D, ROWS)), kept((ROWS, 1))],
        [shape((FF, ROWS), bf16), deep, wide, shape((ROWS, D)), wide, shape((8, D))]
        + [shape((ROWS, D)), wide, shape((D, ROWS), bf16), shape((ROWS, 1))],
        [pltpu.VMEM((ROWS, D), f32)],
        flops=10_000_000_000,
        size=20_000_000,
    )(x, ctx, seg_row, cot, vec, bi, gathered, gathered, gathered)


def backward_one_kernel(dbr, slope, dsec, wi, wb, dpre_o, bi_o, acc):
    b = pl.program_id(0)
    dact = mul(dbr[...], columns(wb, 3, 192, (0, 1)), LAST)
    dpre = (dact * slope[...].astype(f32)).astype(bf16)
    dpre_o[...] = dpre
    bi_o[0:1, :] = column_sum(dpre.astype(f32))
    term = mul(dpre, columns(wi, STEP // LANES), LAST)

    @pl.when(b == 0)
    def _():
        acc[...] = dsec[...] + term

    @pl.when(b > 0)
    def _():
        acc[...] += term


def backward_two_kernel(
    dbr, slope, dsec, wi, wb, wo, n1, inv, vec, dpre_in, bi_in, dpre_o, bi_o, dfirst_o, dattn_o,
    dctx_o, sums_o, acc,
):
    backward_one_kernel(dbr, slope, dsec, wi, wb, dpre_o, bi_o, acc)

    @pl.when(pl.program_id(0) == HALF_STEPS - 1)
    def _():
        grad, normed = acc[...], n1[...]
        sums_o[0:1, :] = column_sum(grad * normed)
        sums_o[1:2, :] = column_sum(grad)
        first = norm_back(grad, normed, inv[...], vec[3:4, :])
        dfirst_o[...] = first
        rounded = first.astype(bf16)
        dattn_o[...] = rounded
        sums_o[2:3, :] = column_sum(rounded.astype(f32))
        dctx_o[...] = mul(rounded, columns(wo, 3, halves=(0, 1)), LAST).astype(bf16)


def backward_specs(half):
    first = HALF_STEPS * half
    ins = [
        whole((ROWS, D)),
        pl.BlockSpec((ROWS, STEP), lambda b: (0, first + b)),
        whole((ROWS, D)),
        pl.BlockSpec((16, 1, STEP * 3 // 8, LANES), lambda b: (0, half, b, 0)),
        pl.BlockSpec((STEP // 192, 2, 576, LANES), lambda b: (first + b, 0, 1, 0)),
    ]
    outs = [
        pl.BlockSpec((ROWS, STEP), lambda b: (0, first + b)),
        pl.BlockSpec((8, STEP), lambda b: (0, first + b)),
    ]
    return ins, outs, [shape((ROWS, FF), bf16), shape((8, FF))]


def backward_one(dbr, slope, dsec, gathered):
    ins, outs, shapes = backward_specs(0)
    return run(
        backward_one_kernel,
        (HALF_STEPS,),
        ins,
        outs + [kept((ROWS, D))],
        shapes + [shape((ROWS, D))],
        flops=5_000_000_000,
        size=10_000_000,
    )(dbr, slope, dsec, gathered, gathered)


def backward_two(dbr, slope, acc, n1, inv, vec, dpre, bi, gathered):
    wide, flat = shape((ROWS, D), bf16), whole((ROWS, D))
    ins, outs, shapes = backward_specs(1)
    return run(
        backward_two_kernel,
        (HALF_STEPS,),
        ins + [OUT, flat, whole((ROWS, 1)), whole((8, D)), ANYWHERE, ANYWHERE],
        outs + [kept((ROWS, D)), kept((ROWS, D)), kept((ROWS, D)), kept((8, D))],
        shapes + [shape((ROWS, D)), wide, wide, shape((8, D))],
        [pltpu.VMEM((ROWS, D), f32)],
        flops=6_000_000_000,
        size=10_000_000,
        alias={9: 0, 10: 1},
    )(dbr, slope, acc, gathered, gathered, gathered, n1, inv, vec, dpre, bi)


def attend_back_kernel(
    half, place, q, k, v, dctx, lse, sr, dfirst, own, other, mixed_o, sums_o, dx_o, bias, acc,
    held, arrived_s,
):
    p = pl.program_id(0)

    @pl.when(p == 0)
    def _():
        bias[...] = jnp.where(upright(sr[...]) == sr[...].astype(f32), 0.0, MASK_FILL)
        acc[...] = dfirst[...]
        for here, source in ((half, own), (1 - half, other)):

            @pl.when(place[3] == here)
            def _():
                copy = pltpu.make_async_copy(source.at[:, :432, :], held, arrived_s.at[0])
                copy.start()
                copy.wait()

    key, value = k[...], v[...]
    turned = key.astype(f32).T.astype(bf16)
    dk = jnp.zeros((ROWS, LANES), f32)
    dv = jnp.zeros((ROWS, LANES), f32)
    parts = []
    for head in range(2):
        query = masked(q[...], head, SCALE)
        grad = masked(dctx[...], head)
        probs = jnp.exp(mul(key, query, LAST) + bias[...] - lse[0, head : head + 1, :])
        dprobs = mul(value, grad, LAST)
        dv = dv + mul(probs.astype(bf16), grad)
        dscores = (probs * (dprobs - column_sum(probs * dprobs))).astype(bf16)
        dk = dk + mul(dscores, query)
        parts.append(mul(turned[64 * head : 64 * (head + 1)], dscores))
    dq = (jnp.concatenate(parts, axis=0).T * SCALE).astype(bf16)
    dk, dv = dk.astype(bf16), dv.astype(bf16)
    mixed_o[0], mixed_o[1], mixed_o[2] = dq, dk, dv
    sums_o[0:1, :] = column_sum(dq.astype(f32))
    sums_o[1:2, :] = column_sum(dv.astype(f32))
    weight = jnp.concatenate([held_columns(held, 3 * t + p) for t in range(3)], axis=1)
    acc[...] += mul(jnp.concatenate([dq, dk, dv], axis=1), weight, LAST)

    @pl.when(p == 2)
    def _():
        dx_o[...] = acc[...].astype(dx_o.dtype)


def attend_back(half, place, q, k, v, dctx, lse, seg_row, dfirst, own, other):
    pair = pl.BlockSpec((ROWS, LANES), lambda p, *_: (0, 3 * half + p))
    return run(
        functools.partial(attend_back_kernel, half),
        (3,),
        [pair, pair, pair, pair, pl.BlockSpec((1, 8, ROWS), lambda p, *_: (3 * half + p, 0, 0))]
        + [whole((1, ROWS)), whole((ROWS, D)), ANYWHERE, ANYWHERE],
        [pl.BlockSpec((3, ROWS, LANES), lambda p, *_: (0, 0, p))]
        + [pl.BlockSpec((8, LANES), lambda p, *_: (0, p)), kept((ROWS, D))],
        [shape((3, ROWS, 384), bf16), shape((8, 384)), shape((ROWS, D), (f32, bf16)[half])],
        [pltpu.VMEM((ROWS, ROWS), f32), pltpu.VMEM((ROWS, D), f32)]
        + [pltpu.VMEM((16, 432, LANES), bf16), pltpu.SemaphoreType.DMA((1,))],
        scalars=1,
        flops=6_000_000_000,
        size=8_000_000,
    )(place, q, k, v, dctx, lse, seg_row, dfirst, own, other)


def put(total, at, grad):
    rows = grad.astype(bf16).reshape(16, 48, -1)
    for j in range(rows.shape[2] // LANES):
        total[:, pl.ds(at + 48 * j, 48), :] = rows[:, :, LANES * j : LANES * (j + 1)]


def back_grad_kernel(place, act, act_2, dbr, dbr_2, total):
    grad = (mul(act[...], dbr[...]) + mul(act_2[...], dbr_2[...])).astype(bf16)
    for at in range(2):
        for j in range(3):
            part = grad[192 * at : 192 * (at + 1), LANES * j : LANES * (j + 1)]
            total[at, 192 * j : 192 * (j + 1), :] = part

def back_grad(place, act, act_2, dbr, dbr_2):
    tall = pl.BlockSpec((384, ROWS), lambda b, p: (b, 0))
    half = pl.BlockSpec((ROWS, 384), lambda b, p: (0, p[3]))
    return run(
        back_grad_kernel,
        (8,),
        [tall, tall, half, half],
        pl.BlockSpec((2, 576, LANES), lambda b, p: (b, 0, 0)),
        shape((16, 576, LANES), bf16),
        scalars=1,
        flops=2_400_000_000,
        size=10_000_000,
    )(place, act, act_2, dbr, dbr_2)


def middle_grad_kernel(
    place, low, low_2, dpre, dpre_2, ctx, ctx_2, dattn, dattn_2, two, bi, one, total
):
    b = pl.program_id(0)

    @pl.when(b < 4)
    def _():
        grad = mul(low[...], dpre[...]) + mul(low_2[...], dpre_2[...])
        put(total, pl.multiple_of(144 * b, 16), grad)

    @pl.when(b == 4)
    def _():
        put(total, 576, mul(ctx[...], dattn[...]) + mul(ctx_2[...], dattn_2[...]))
        names = (("g2", two, 0), ("s2", two, 1), ("bb", two, 2), ("bi", bi, 0))
        names = names + (("g1", one, 0), ("s1", one, 1), ("bo", one, 2))
        total[:, 720:736, :] = gathered_rows([(n, ref[i : i + 1, :]) for n, ref, i in names])


def middle_grad(place, low, low_2, dpre, dpre_2, ctx, ctx_2, dattn, dattn_2, two, bi, one):
    tall = whole((D, ROWS))
    quarter = pl.BlockSpec((ROWS, 384), lambda b, p: (0, 4 * p[3] + jnp.minimum(b, 3)))
    half = pl.BlockSpec((ROWS, 384), lambda b, p: (0, p[3]))
    return run(
        middle_grad_kernel,
        (5,),
        [tall, tall, quarter, quarter, tall, tall, half, half]
        + [whole((8, D)), whole((8, FF)), whole((8, D))],
        kept((16, 736, LANES)),
        shape((16, 736, LANES), bf16),
        scalars=1,
        flops=3_200_000_000,
        size=12_000_000,
    )(place, low, low_2, dpre, dpre_2, ctx, ctx_2, dattn, dattn_2, two, bi, one)


def qkv_grad_kernel(place, x, x_2, left, left_2, right, right_2, sums_l, sums_r, total):
    for core, own, other in ((0, left, left_2), (1, right, right_2)):

        @pl.when(place[3] == core)
        def _():
            for t in range(3):
                put(total, 144 * t, mul(x[...], own[t]) + mul(x_2[...], other[t]))

    sums = [jnp.concatenate([sums_l[i : i + 1, :], sums_r[i : i + 1, :]], axis=1) for i in (0, 1)]
    total[:, 432:448, :] = gathered_rows([("bq", sums[0]), ("bv", sums[1])])


def qkv_grad(place, x, x_2, left, left_2, right, right_2, sums_l, sums_r):
    half = kept((3, ROWS, 384))
    return run(
        qkv_grad_kernel,
        (1,),
        [kept((D, ROWS)), kept((D, ROWS)), half, half, half, half, kept((8, 384)), kept((8, 384))],
        kept((16, 448, LANES)),
        shape((16, 448, LANES), bf16),
        scalars=1,
        flops=1_800_000_000,
        size=7_000_000,
    )(place, x, x_2, left, left_2, right, right_2, sums_l, sums_r)


def last_kernel(place, *refs):
    late, outs = refs[5], refs[6:]
    back, middle = refs[0][...].astype(f32), refs[4][...].astype(f32)
    for part in refs[1:4]:
        back = back + part[...].astype(f32)
    qkv = late[0].astype(f32)
    for i in range(1, 16):
        qkv = qkv + late[i].astype(f32)
    wide = [qkv[48 * j : 48 * (j + 1)] for j in range(9)]
    wide = wide + [middle[576 + 48 * j : 576 + 48 * (j + 1)] for j in range(3)]
    wide = wide + [middle[48 * j : 48 * (j + 1)] for j in range(12)]
    rows = middle[720:728] + qkv[432:440]
    none = jnp.zeros((4, LANES), f32)
    for z in range(4):
        parts = []
        for block in wide:
            parts = parts + [block[12 * z : 12 * (z + 1)], none]
        for j in range(3):
            parts.append(back[192 * j + 48 * z : 192 * j + 48 * (z + 1)])
        parts = parts + [rows[2 * z : 2 * (z + 1)], jnp.zeros((14, LANES), f32)]
        total = jnp.concatenate(parts, axis=0).astype(bf16)
        for k in range(4):

            @pl.when((place[2] + k) % 4 == z)
            def _():
                outs[k][...] = total


def last_sum(place, parts):
    return run(
        last_kernel,
        (1,),
        [kept(p.shape) for p in parts],
        [kept((544, LANES))] * 4,
        [shape((544, LANES), bf16)] * 4,
        scalars=1,
        size=4_000_000,
    )(place, *parts)


def around(parts, axis):
    return [parts[0]] + [lax.ppermute(parts[k], axis, shifted(4, k)) for k in (1, 3, 2)]


def scattered(value, axis):
    return lax.psum_scatter(value, axis, tiled=True)


def swap(value):
    return lax.ppermute(value, "c", shifted(2, 1))


def together(*values):
    flat, tree = jax.tree.flatten(values)
    return jax.tree.unflatten(tree, lax.optimization_barrier(tuple(flat)))


def assemble_kernel(place, own, other, qkv, out, inw, back, row):
    mine, theirs = own[...], other[...].astype(f32)
    row[...] = mine[216:217] + theirs[216:217]
    for core in range(2):

        @pl.when(place[3] == core)
        def _():
            for half, rows in ((core, mine), (1 - core, theirs)):
                blocks = [(qkv, 6 * t + 3 * half + j) for t in range(3) for j in range(3)]
                blocks += [(out, 3 * half + j) for j in range(3)]
                blocks += [(inw, 12 * half + j) for j in range(12)]
                for i, (ref, j) in enumerate(blocks):
                    ref[:, LANES * j : LANES * (j + 1)] = rows[6 * i : 6 * (i + 1)]
                for i in range(3):
                    j = 3 * half + i
                    part = rows[144 + 24 * i : 144 + 24 * (i + 1)]
                    back[:, LANES * j : LANES * (j + 1)] = part


def assemble(place, own, other):
    outs = [(6, 3 * D), (6, D), (6, FF), (24, D), (1, LANES)]
    return run(
        assemble_kernel,
        (1,),
        [kept((224, LANES))] * 2,
        [kept(o) for o in outs],
        [shape(o) for o in outs],
        scalars=1,
    )(place, own, other)


def finish(place, core, parts):
    parts = around(last_sum(place, parts), "z")
    total = sum(p.astype(f32) for p in parts)
    wide = total[:384].reshape(24, 16, LANES)[:, :12].reshape(24, 2, 6, LANES)
    tall = total[384:528].reshape(3, 2, 24, LANES)

    def for_core(which):
        a = lax.dynamic_index_in_dim(wide, which, 1, keepdims=False).reshape(144, LANES)
        b = lax.dynamic_index_in_dim(tall, which, 1, keepdims=False).reshape(72, LANES)
        row = lax.dynamic_index_in_dim(total[528:530], which, 0)
        return jnp.concatenate([a, b, row, jnp.zeros((7, LANES), f32)], axis=0)

    own = for_core(core)
    other = swap(for_core(1 - core).astype(bf16))
    *weights, rows = assemble(place, own, other)
    return weights, {n: rows[0, AT[n] : AT[n] + CUTS[n]] for n in NAMES}


def segment_rows(lengths, assignment, device, rows):
    count = lengths.shape[0]
    order = jnp.arange(count, dtype=jnp.int32)
    same = assignment[:, None] == assignment[None, :]
    before = order[None, :] < order[:, None]
    offset = jnp.sum(jnp.where(same & before, lengths[None, :], 0), axis=1)
    places = jnp.arange(rows, dtype=jnp.int32)[:, None]
    inside = (
        (assignment[None, :] == device)
        & (places >= offset[None, :])
        & (places < (offset + lengths)[None, :])
    )
    return jnp.sum(jnp.where(inside, order[None, :] + 1, 0), axis=1)


def body(
    hidden_in,
    out_cotangent,
    lengths,
    assignment,
    qkv_weight,
    query_bias,
    value_bias,
    out_weight,
    out_bias,
    first_gain,
    first_shift,
    in_weight,
    in_bias,
    back_weight,
    back_bias,
    second_gain,
    second_shift,
):
    small = [
        query_bias,
        value_bias,
        out_bias,
        first_gain,
        first_shift,
        in_bias,
        back_bias,
        second_gain,
        second_shift,
    ]
    px, py, pz, core = (lax.axis_index(a) for a in ("x", "y", "z", "c"))
    place = jnp.stack([px, py, pz, core]).astype(jnp.int32)
    segment = segment_rows(lengths, assignment, ((px * 4 + py) * 4 + pz) * 2 + core, ROWS)
    seg_row = segment.reshape(1, ROWS)
    ready = (hidden_in.T, seg_row)
    own, other, gathered, ready = gather_all(
        place, qkv_weight, out_weight, in_weight, back_weight, small, ready
    )
    turned, seg_row = ready
    q, k, v, lse, ctx_rows, ctx, vec, bi = attend(
        place, hidden_in, seg_row, own, other
    )
    turned_2, ctx_2 = swap(turned), swap(ctx)
    act, slope, layer_out, dsec, dbr, two, n1, low, low_t, inv = forward(
        hidden_in, ctx_rows, seg_row, out_cotangent, vec, bi, gathered
    )
    act, dbr, turned_2, ctx_2 = together(act, dbr, turned_2, ctx_2)
    act_2, dbr_2, low_2 = swap(act), swap(dbr), swap(low_t)
    dpre, dbi, acc = backward_one(dbr, slope, dsec, gathered)
    act_2, dbr_2, low_2, acc = together(act_2, dbr_2, low_2, acc)
    back = back_grad(place, act, act_2, dbr, dbr_2)
    back, acc = together(back, acc)
    back = scattered(back.reshape(-1, LANES), "x")
    dpre, dbi, dfirst, dattn, dctx, one = backward_two(
        dbr, slope, acc, n1, inv, vec, dpre, dbi, gathered
    )
    dpre_2, dattn_2 = swap(dpre), swap(dattn)
    middle = middle_grad(
        place, low_t, low_2, dpre, dpre_2, ctx, ctx_2, dattn, dattn_2, two, dbi, one
    )
    middle, dctx = together(middle, dctx)
    middle = scattered(middle.reshape(-1, LANES), "x")
    left, sums_l, acc = attend_back(
        0, place, q, k, v, dctx, lse, seg_row, dfirst, own, other
    )
    left_2 = swap(left)
    blocks = back.reshape(4, 576, LANES)
    back = [lax.dynamic_index_in_dim(blocks, (py + k) % 4, 0, keepdims=False) for k in range(4)]
    back, acc = together(back, acc)
    back = around(back, "y")
    right, sums_r, input_grad = attend_back(
        1, place, q, k, v, dctx, lse, seg_row, acc, own, other
    )
    left_2, back, right = together(left_2, back, right)
    right_2, middle = together(swap(right), middle)
    late = qkv_grad(place, turned, turned_2, left, left_2, right, right_2, sums_l, sums_r)
    parts = [*back, scattered(middle, "y"), lax.all_to_all(late, ("x", "y"), 0, 0, tiled=True)]
    weights, s = finish(place, core, parts)
    return (
        layer_out,
        input_grad,
        weights[0],
        s["bq"],
        s["bv"],
        weights[1],
        s["bo"],
        s["g1"],
        s["s1"],
        weights[2],
        s["bi"],
        weights[3],
        s["bb"],
        s["g2"],
        s["s2"],
    )


def solution(mesh):
    axes = ("x", "y", "z", "c")
    grid = Mesh(mesh.devices.reshape(4, 4, 4, 2), axes)
    two, one, every = P(axes, None), P(axes), P()
    in_specs = (two, two, every, every, two, one, one, two, one, one, one, two, one, two)
    in_specs = in_specs + (one, one, one)
    out_specs = (two, two, two, one, one, two, one, one, one, two, one, two, one, one, one)
    return jax.shard_map(body, mesh=grid, in_specs=in_specs, out_specs=out_specs, check_vma=False)
```
